128 devices in a mesh: patch: 32 (over z, y, core), lev: 4 (over x).
Axes of the slice: x: 4, y: 4, z: 4, core: 2. Of those that a mesh axis runs over, the one named last changes fastest.
Arguments:
- background: bfloat16 [128, 4, 512, 6, 256], P('patch', 'lev'), may hold values from -6 to 6
- patch_order: int32 [512], replicated, may hold values from 0 to 511, each once
- tile_counts: int32 [512], P('patch'), may hold values from 1 to 49, as said below
- obs_column: int32 [262144], P('patch'), may hold values from 0 to 255
- obs_operator: bfloat16 [4, 6, 262144], P(None, None, 'patch'), may hold values from -1.25 to 1.25
- obs_value: float32 [262144], P('patch'), may hold values from -6 to 6
- obs_weight: float32 [262144], P('patch'), may hold values from 0.05 to 2
Outputs:
- analysis: bfloat16 [128, 4, 512, 6, 256], P('patch', 'lev')
The draws below stay inside these ranges and needn't reach their ends.
Inputs may be any that keep to these rules, and one draw needn't show every extreme that they name: `tile_counts`: the entries 16 g to 16 g + 15 sum to at most 64 for every g, and to exactly 64 for some g; no entry exceeds 64 - 15, and some entry equals it.
All inputs are finite; a program needn't handle non-finite values.
Results may differ from the reference program's by a relative error of at most 0.0056.
Values may be sent and summed in bfloat16 or wider, within the bound.
No kernel may reach another device: no remote copies, remote signals or barrier semaphores. Data moves between devices by JAX's collectives and lax.ppermute only.
A program may use at most 128 MiB of HBM per device.

```python
import math
import jax
import jax.numpy as jnp
from jax import lax

K = 128
CP = 256
F = 6
TILE = 128
ITERS = 10
P_DEV = 16
TILES_DEV = 64
OBS_DEV = 8192
P_SIZE = 512
OBS = 262144
LP = 4
N_PATCH = 32


def draw_tile_counts(key, part):
    key = jax.random.fold_in(key, 11)
    first, second, third = jax.random.split(key, 3)
    groups = P_SIZE // P_DEV
    used = jax.random.randint(first, (groups,), TILES_DEV // 2, TILES_DEV + 1)
    filled = jax.random.randint(second, (), 0, groups)
    used = jnp.where(jnp.arange(groups) == filled, TILES_DEV, used)
    shares = jax.random.randint(third, (groups, P_DEV), 1, 5) ** 3
    extra = used - P_DEV
    blocks = 1 + extra[:, None] * shares // jnp.sum(shares, axis=1, keepdims=True)
    leftover = used - jnp.sum(blocks, axis=1)
    heavy = jnp.argmax(shares, axis=1)
    is_heavy = jnp.arange(P_DEV)[None, :] == heavy[:, None]
    blocks = blocks + jnp.where(is_heavy, leftover[:, None], 0)
    single = jnp.where(is_heavy, TILES_DEV - P_DEV + 1, 1)
    blocks = jnp.where((jnp.arange(groups) == filled)[:, None], single, blocks)
    return blocks.reshape(P_SIZE).astype(jnp.int32)


def touch_ends(values, rng, least, high):
    longest = values.shape.index(max(values.shape))
    spots = []
    for shift in (0, 1):
        where = [jax.random.randint(jax.random.fold_in(rng, axis), (), 0, length) for axis, length in enumerate(values.shape)]
        where[longest] = (where[longest] + shift) % values.shape[longest]
        spots.append(tuple(where))
    return values.at[spots[0]].set(least).at[spots[1]].set(high)


def shard_levels(rng, shape, cuts, least, largest):
    gain = 1.0
    for dim, shards_of in cuts:
        draws = jax.random.uniform(jax.random.fold_in(jax.random.fold_in(rng, 6), dim), (shards_of,), jnp.float32, least / len(cuts), largest / len(cuts))
        gain = gain * jnp.repeat(jnp.exp(draws), shape[dim] // shards_of).reshape((-1,) + (1,) * (len(shape) - 1 - dim))
    return gain


def noise(rng, extent, deviation, reach, cuts=(), kind=jnp.bfloat16):
    array = jax.random.normal(rng, extent, jnp.float32) * deviation
    if len(cuts) > 0:
        array = shard_levels(rng, extent, cuts, -0.22, 0.18) * array
    return jnp.clip(array, min=-reach, max=reach).astype(kind)


def setup_inputs(seed: int = 0) -> dict:
    streams_of = jax.random.split(jax.random.key(seed), 8)
    return {
        "background": noise(streams_of[0], (K, LP, P_SIZE, F, CP), 1.0, 6.0, ((0, 32), (1, 4))),
        "patch_order": jax.random.permutation(streams_of[1], P_SIZE).astype(jnp.int32),
        "tile_counts": draw_tile_counts(jax.random.fold_in(streams_of[7], 71), 0),
        "obs_column": touch_ends(jax.random.randint(streams_of[3], (OBS,), 0, CP), jax.random.fold_in(streams_of[3], 1), 0, CP - 1).astype(jnp.int32),
        "obs_operator": noise(streams_of[4], (LP, F, OBS), (LP * F) ** -0.5, 1.25, ((2, 32),)),
        "obs_value": noise(streams_of[5], (OBS,), 1.0, 6.0, ((0, 32),), jnp.float32),
        "obs_weight": jnp.clip(jnp.exp(math.log(2.0) - 3.6888794 * jax.random.uniform(streams_of[6], (OBS,), jnp.float32) ** shard_levels(streams_of[6], (OBS,), ((0, 32),), -0.2, 0.2)), 0.05, 2.0),
    }


HIGH = lax.Precision.HIGHEST

def tile_slots(counts, tiles):
    block_ends = jnp.cumsum(counts)
    tile_index = jnp.arange(tiles, dtype=jnp.int32)
    slots = lax.optimization_barrier(jnp.sum((block_ends[None, :] <= tile_index[:, None]).astype(jnp.int32), axis=1))
    return (slots, tile_index < block_ends[-1])

def gram_terms(observed, obs_value, row_weight, tiles):
    members = observed.shape[0]
    ymean = lax.optimization_barrier(jnp.mean(observed, axis=0))
    ypert = observed - ymean[None, :]
    depart = obs_value - ymean
    scaled = ypert * row_weight[None, :]
    ypert_tiles = ypert.reshape(members, tiles, -1)
    scaled_tiles = scaled.reshape(members, tiles, -1)
    tile_gram = jnp.einsum('kto,jto->tkj', scaled_tiles, ypert_tiles, precision=HIGH)
    tile_rhs = jnp.einsum('kto,to->tk', scaled_tiles, depart.reshape(tiles, -1), precision=HIGH)
    return (tile_gram, tile_rhs)

def solve_weights(gram, rhs):
    members = gram.shape[1]
    eye = jnp.eye(members, dtype=jnp.float32)
    system = gram + (members - 1.0) * eye[None]
    scale = jnp.sqrt(lax.optimization_barrier(jnp.sum(system * system, axis=(1, 2))))
    upper = system / scale[:, None, None]
    lower = jnp.broadcast_to(eye, system.shape)
    for _ in range(ITERS):
        middle = 1.5 * eye[None] - 0.5 * jnp.matmul(lower, upper, precision=HIGH)
        upper = jnp.matmul(upper, middle, precision=HIGH)
        lower = jnp.matmul(middle, lower, precision=HIGH)
    root_inv = lower / jnp.sqrt(scale)[:, None, None]
    inner = jnp.einsum('sjk,sk->sj', root_inv, rhs, precision=HIGH)
    wmean = jnp.einsum('sjk,sk->sj', root_inv, inner, precision=HIGH)
    weights = jnp.sqrt(members - 1.0) * root_inv + wmean[:, :, None]
    return weights.astype(jnp.bfloat16)

def apply_weights(states, weights):
    state_mean = lax.optimization_barrier(jnp.mean(states.astype(jnp.float32), axis=0, keepdims=True))
    xpert = (states.astype(jnp.float32) - state_mean).astype(jnp.bfloat16)
    mixed = jnp.einsum('jlsfc,sjk->klsfc', xpert.astype(jnp.float32), weights.astype(jnp.float32))
    return (state_mean + mixed).astype(jnp.bfloat16)

def reference(background, patch_order, tile_counts, obs_column, obs_operator, obs_value, obs_weight):

    def one_group(group):
        order = lax.dynamic_slice_in_dim(patch_order, group * P_DEV, P_DEV)
        counts = lax.dynamic_slice_in_dim(tile_counts, group * P_DEV, P_DEV)
        column = lax.dynamic_slice_in_dim(obs_column, group * OBS_DEV, OBS_DEV)
        operator = lax.dynamic_slice_in_dim(obs_operator, group * OBS_DEV, OBS_DEV, 2)
        values = lax.dynamic_slice_in_dim(obs_value, group * OBS_DEV, OBS_DEV)
        weight = lax.dynamic_slice_in_dim(obs_weight, group * OBS_DEV, OBS_DEV)
        patches = jnp.take(background, order, axis=2)
        slots, live = tile_slots(counts, TILES_DEV)
        slot_rows = jnp.repeat(jnp.minimum(slots, P_DEV - 1), TILE)
        live_rows = jnp.repeat(live, TILE).astype(jnp.float32)
        picked = patches[:, :, slot_rows, :, column]
        observed = jnp.einsum('oklf,lfo->ko', picked.astype(jnp.float32), operator.astype(jnp.float32))
        tile_gram, tile_rhs = gram_terms(observed, values, weight * live_rows, TILES_DEV)
        onehot = ((slots[None, :] == jnp.arange(P_DEV, dtype=jnp.int32)[:, None]) & live[None, :]).astype(jnp.float32)
        gram = jnp.einsum('st,tkj->skj', onehot, tile_gram, precision=HIGH)
        rhs = jnp.dot(onehot, tile_rhs, precision=HIGH)
        weights = solve_weights(gram, rhs)
        return apply_weights(patches, weights)
    result = lax.map(one_group, jnp.arange(N_PATCH, dtype=jnp.int32))
    result = jnp.transpose(result, (1, 2, 0, 3, 4, 5)).reshape(K, LP, P_SIZE, F, CP)
    inverse = jnp.zeros((P_SIZE,), jnp.int32).at[patch_order].set(jnp.arange(P_SIZE, dtype=jnp.int32))
    return jnp.take(result, inverse, axis=2)
```

```python
import functools

import jax
import jax.numpy as jnp
from jax import lax
from jax.experimental import pallas as pl
from jax.experimental.pallas import tpu as pltpu
from jax.sharding import PartitionSpec as P

TILE = 128
ITERS = 10
CHUNKS = (16,)
F32 = jnp.float32
BF16 = jnp.bfloat16
VMEM_LIMIT = 56 * 1024 * 1024
AUG = 16


def params(semantics=None):
    return pltpu.CompilerParams(vmem_limit_bytes=VMEM_LIMIT, dimension_semantics=semantics)


def vmem():
    return pl.BlockSpec(memory_space=pltpu.VMEM)


def smem():
    return pl.BlockSpec(memory_space=pltpu.SMEM)


def dot(a, b):
    return jnp.dot(a, b, preferred_element_type=F32)


def dot_nt(a, b):
    return lax.dot_general(a, b, (((1,), (1,)), ((), ())), preferred_element_type=F32)


def split(a):
    hi = a.astype(BF16)
    return hi, (a - hi.astype(F32)).astype(BF16)


def dot3(a, b, mul=dot):
    ah, al = a
    bh, bl = b
    return mul(ah, bh) + (mul(ah, bl) + mul(al, bh))


def send_kernel(hot_ref, x_ref, out_ref):
    groups, rows, cols = out_ref.shape[0], out_ref.shape[2], out_ref.shape[3]
    members = x_ref.shape[0]
    slots = rows // members
    hot = hot_ref[...]
    parts = [
        dot(hot, x_ref[m, 0]).reshape(groups, slots, cols) for m in range(members)
    ]
    out_ref[:, 0] = jnp.concatenate(parts, axis=1).astype(BF16)


def send(hot, x, slots):
    members, fields, patches, cols = x.shape
    groups = hot.shape[0] // slots
    return pl.pallas_call(
        send_kernel,
        grid=(fields,),
        in_specs=[
            pl.BlockSpec(hot.shape, lambda f: (0, 0)),
            pl.BlockSpec((members, 1, patches, cols), lambda f: (0, f, 0, 0)),
        ],
        out_specs=pl.BlockSpec((groups, 1, members * slots, cols), lambda f: (0, f, 0, 0)),
        out_shape=jax.ShapeDtypeStruct((groups, fields, members * slots, cols), BF16),
        compiler_params=params(),
        name="send_permute",
    )(hot, x)


def observe_kernel(first, counts_ref, perm_ref, recv_ref, op_ref, col_ref, x_ref, y_ref):
    groups, fields, rows, cols = recv_ref.shape
    slots, members = x_ref.shape[0], x_ref.shape[1]
    gather = perm_ref.shape[0] // rows
    part = members * gather // groups
    perm = perm_ref[...]

    def reorder(f, carry):
        for b in range(groups // gather):
            block = recv_ref[b * gather : (b + 1) * gather, f].reshape(gather * rows, cols)
            moved = dot(perm, block).astype(BF16).reshape(slots, part, cols)
            x_ref[:, b * part : (b + 1) * part, pl.ds(pl.multiple_of(f * cols, cols), cols)] = moved
        return carry

    lax.fori_loop(0, fields, reorder, 0)

    start = jnp.int32(0)
    for s in range(first):
        start = start + counts_ref[s]
    column_ids = lax.broadcasted_iota(jnp.int32, (cols, TILE), 0)

    def slot_step(s, base):
        count = counts_ref[first + s]

        def tile_step(i, carry):
            local = base + i
            row = start + local
            hit = (column_ids == col_ref[pl.ds(row, 1), :]).astype(BF16)
            weights = op_ref[row]
            table = jnp.concatenate(
                [hit * weights[f : f + 1, :].astype(BF16) for f in range(fields)], axis=0
            )
            y = dot(x_ref[s], table)
            mean = jnp.mean(y, axis=0, keepdims=True)
            hi = mean.astype(BF16).astype(F32)
            mid = (mean - hi).astype(BF16).astype(F32)
            tail = jnp.concatenate(
                [hi, mid, mean - hi - mid, jnp.zeros((AUG - 3, TILE), F32)], axis=0
            )
            lev = lax.rem(local, 4)
            y_ref[lev, lax.div(local, 4), 0:members, :] = (y - mean).astype(BF16)
            y_ref[lev, lax.div(local, 4), members : members + AUG, :] = tail.astype(BF16)
            return carry

        lax.fori_loop(0, count, tile_step, 0)
        return base + count

    lax.fori_loop(0, slots, slot_step, jnp.int32(0))


def observe(counts, perm, recv, op, col, first, slots, tiles):
    groups, fields, rows, cols = recv.shape
    members = groups * rows // slots
    return pl.pallas_call(
        functools.partial(observe_kernel, first),
        in_specs=[smem(), vmem(), vmem(), vmem(), vmem()],
        out_specs=[vmem(), vmem()],
        out_shape=[
            jax.ShapeDtypeStruct((slots, members, fields * cols), BF16),
            jax.ShapeDtypeStruct((4, tiles // 4, members + AUG, TILE), BF16),
        ],
        compiler_params=params(),
        name="observe",
    )(counts, perm, recv, op, col)


def gram_kernel(first, counts_ref, lev_ref, y_ref, value_ref, weight_ref, out_ref):
    slots = out_ref.shape[0] * out_ref.shape[1]
    per = out_ref.shape[1]
    members = out_ref.shape[3]
    lev = lev_ref[0]
    out_ref[...] = jnp.zeros_like(out_ref)
    start = jnp.int32(0)
    for s in range(first):
        start = start + counts_ref[s]
    base = jnp.int32(0)
    for s in range(slots):
        count = counts_ref[first + s]

        def tile_step(i, carry, s=s):
            row = start + 4 * i + lev
            total = y_ref[0, i].astype(F32)
            for l in range(1, 4):
                total = total + y_ref[l, i].astype(F32)
            pert = total[0:members]
            mean = total[members : members + 1] + (
                total[members + 1 : members + 2] + total[members + 2 : members + 3]
            )
            weight = weight_ref[pl.ds(row, 1), :]
            depart = value_ref[pl.ds(row, 1), :] - mean
            aug = jnp.concatenate([pert, depart, jnp.zeros((AUG - 1, TILE), F32)], axis=0)
            out_ref[s // per, s % per] += dot3(split(aug * weight), split(pert), dot_nt)
            return carry

        lax.fori_loop(
            lax.div(base - lev + 3, 4), lax.div(base + count - lev + 3, 4), tile_step, 0
        )
        base = base + count


def partial_gram(counts, lev, y, value, weight, first, slots):
    members = y.shape[2] - AUG
    return pl.pallas_call(
        functools.partial(gram_kernel, first),
        in_specs=[smem(), smem(), vmem(), vmem(), vmem()],
        out_specs=vmem(),
        out_shape=jax.ShapeDtypeStruct((4, slots // 4, members + AUG, members), F32),
        compiler_params=params(),
        name="gram",
    )(counts, lev, y, value, weight)


def solve_kernel(g_ref, out_ref):
    slots, members = out_ref.shape[0], out_ref.shape[1]
    row = lax.broadcasted_iota(jnp.int32, (members, members), 0)
    eye = (row == lax.broadcasted_iota(jnp.int32, (members, members), 1)).astype(F32)
    uppers, lowers, scales, sides = [], [], [], []
    for s in range(slots):
        total = (g_ref[0, s] + g_ref[1, s]) + (g_ref[2, s] + g_ref[3, s])
        system = total[0:members] + (members - 1.0) * eye
        square = jnp.sum(jnp.sum(system * system, axis=1, keepdims=True), axis=0, keepdims=True)
        scale = jnp.sqrt(square)
        uppers.append(system / scale)
        lowers.append(eye)
        scales.append(scale)
        sides.append(total[members : members + 8])

    for step in range(ITERS):
        for s in range(slots):
            upper = split(uppers[s])
            if step == 0:
                middle = 1.5 * eye - 0.5 * uppers[s]
                lowers[s] = middle
                uppers[s] = dot3(upper, split(middle))
                continue
            lower = split(lowers[s])
            middle = split(1.5 * eye - 0.5 * dot3(lower, upper))
            lowers[s] = dot3(middle, lower)
            if step < ITERS - 1:
                uppers[s] = dot3(upper, middle)
    for s in range(slots):
        root = lowers[s] / jnp.sqrt(scales[s])
        parts = split(root)
        inner = dot3(split(sides[s]), parts, dot_nt)
        wmean = dot3(split(inner), parts, dot_nt)[0:1]
        out_ref[s] = (jnp.sqrt(jnp.float32(members - 1.0)) * root + wmean).astype(BF16)


def solve(g):
    members = g.shape[3]
    return pl.pallas_call(
        solve_kernel,
        in_specs=[vmem()],
        out_specs=vmem(),
        out_shape=jax.ShapeDtypeStruct((g.shape[1], members, members), BF16),
        compiler_params=params(),
        name="newton_schulz",
    )(g)


def apply_kernel(perm_ref, w_ref, x_ref, out_ref, mixed_ref):
    slots, members, cols = x_ref.shape
    groups, rows = out_ref.shape[0], out_ref.shape[2]
    gather = perm_ref.shape[0] // rows
    part = members * gather // groups
    for s in range(slots):
        x = x_ref[s].astype(F32)
        mean = jnp.mean(x, axis=0, keepdims=True)
        mixed = dot(w_ref[s], (x - mean).astype(BF16))
        mixed_ref[s] = (mean + mixed).astype(BF16)
    perm = perm_ref[...]
    for b in range(groups // gather):
        block = mixed_ref[:, b * part : (b + 1) * part, :].reshape(slots * part, cols)
        moved = dot(perm, block).astype(BF16).reshape(gather, rows, cols)
        out_ref[b * gather : (b + 1) * gather, 0] = moved


def apply(perm, w, x, groups, fields):
    slots, members, width = x.shape
    cols = width // fields
    rows = slots * members // groups
    return pl.pallas_call(
        apply_kernel,
        grid=(fields,),
        in_specs=[
            pl.BlockSpec(perm.shape, lambda f: (0, 0)),
            pl.BlockSpec(w.shape, lambda f: (0, 0, 0)),
            pl.BlockSpec((slots, members, cols), lambda f: (0, 0, f)),
        ],
        out_specs=pl.BlockSpec((groups, 1, rows, cols), lambda f: (0, f, 0, 0)),
        out_shape=jax.ShapeDtypeStruct((groups, fields, rows, cols), BF16),
        scratch_shapes=[pltpu.VMEM((slots, members, cols), BF16)],
        compiler_params=params(),
        name="apply_weights",
    )(perm, w, x)


def restore_kernel(hot_ref, *refs):
    out_ref = refs[-1]
    members = out_ref.shape[0]
    blocks = [ref[:, 0].astype(F32) for ref in refs[:-1]]
    for m in range(members):
        parts = []
        for block in blocks:
            groups, rows, cols = block.shape
            slots = rows // members
            parts.append(block[:, m * slots : (m + 1) * slots].reshape(groups * slots, cols))
        stacked = jnp.concatenate(parts, axis=0).astype(BF16)
        out_ref[m, 0] = dot(hot_ref[...], stacked).astype(BF16)


def restore(hot, recvs, members):
    fields, cols = recvs[0].shape[1], recvs[0].shape[3]
    patches = hot.shape[0]
    specs = [
        pl.BlockSpec((r.shape[0], 1, r.shape[2], cols), lambda f: (0, f, 0, 0)) for r in recvs
    ]
    return pl.pallas_call(
        restore_kernel,
        grid=(fields,),
        in_specs=[pl.BlockSpec(hot.shape, lambda f: (0, 0))] + specs,
        out_specs=pl.BlockSpec((members, 1, patches, cols), lambda f: (0, f, 0, 0)),
        out_shape=jax.ShapeDtypeStruct((members, fields, patches, cols), BF16),
        compiler_params=params(),
        name="restore_order",
    )(hot, *recvs)


def row_permutation(slots, members_local, gather):
    size = slots * members_local * gather
    target = jnp.arange(size, dtype=jnp.int32)
    slot, rest = target // (gather * members_local), target % (gather * members_local)
    origin = rest * slots + slot
    return (origin[:, None] == jnp.arange(size, dtype=jnp.int32)[None, :]).astype(BF16)


def body(background, patch_order, tile_counts, obs_column, obs_operator, obs_value, obs_weight):
    members_local, _, patches, fields, columns = background.shape
    slots_dev = tile_counts.shape[0]
    groups = patches // slots_dev
    tiles = obs_column.shape[0] // TILE
    level = lax.axis_index("lev")
    lev = jnp.reshape(level, (1,)).astype(jnp.int32)
    x = jnp.transpose(background[:, 0], (0, 2, 1, 3))
    order = patch_order.reshape(groups, slots_dev)
    ids = jnp.arange(patches, dtype=jnp.int32)
    col = obs_column.reshape(tiles, TILE)
    value = obs_value.reshape(tiles, TILE)
    weight = obs_weight.reshape(tiles, TILE)
    op = lax.dynamic_index_in_dim(obs_operator, level, 0, keepdims=False)
    op = jnp.transpose(op.reshape(fields, tiles, TILE), (1, 0, 2)).astype(F32)
    op = jnp.pad(op, ((0, 0), (0, 8 - fields), (0, 0)))

    orders, gathered, firsts = [], [], []
    first = 0
    for slots in CHUNKS:
        part = order[:, first : first + slots].reshape(-1)
        hot = (part[:, None] == ids[None, :]).astype(BF16)
        sent = send(hot, x, slots)
        orders.append(part)
        gathered.append(lax.all_to_all(sent, "patch", split_axis=0, concat_axis=0, tiled=True))
        firsts.append(first)
        first += slots

    backs = []
    for slots, first, recv in zip(CHUNKS, firsts, gathered):
        gather = 256 // (slots * members_local)
        perm = row_permutation(slots, members_local, gather)
        room = tiles - (slots_dev - slots)
        states, y = observe(tile_counts, perm, recv, op, col, first, slots, room)
        y = lax.all_to_all(y, "lev", split_axis=0, concat_axis=0, tiled=True)
        g = partial_gram(tile_counts, lev, y, value, weight, first, slots)
        g = lax.all_to_all(g, "lev", split_axis=0, concat_axis=0, tiled=True)
        w = solve(g)
        w = lax.all_to_all(
            jnp.broadcast_to(w[None], (4,) + w.shape), "lev", split_axis=0, concat_axis=0, tiled=True
        ).reshape(slots, w.shape[1], w.shape[2])
        out = apply(perm.T, w, states, groups, fields)
        backs.append(lax.all_to_all(out, "patch", split_axis=0, concat_axis=0, tiled=True))

    merged = jnp.concatenate(orders)
    hot = (ids[:, None] == merged[None, :]).astype(BF16)
    result = restore(hot, backs, members_local)
    return jnp.transpose(result, (0, 2, 1, 3))[:, None]


def solution(mesh):
    in_specs = (
        P("patch", "lev", None, None, None),
        P(),
        P("patch"),
        P("patch"),
        P(None, None, "patch"),
        P("patch"),
        P("patch"),
    )
    out_specs = P("patch", "lev", None, None, None)
    return jax.shard_map(body, mesh=mesh, in_specs=in_specs, out_specs=out_specs, check_vma=False)
```

```python
import functools

import jax
import jax.numpy as jnp
from jax import lax
from jax.experimental import pallas as pl
from jax.experimental.pallas import tpu as pltpu
from jax.sharding import PartitionSpec as P

TILE = 128
ITERS = 10
CHUNKS = (8, 8)
F32 = jnp.float32
BF16 = jnp.bfloat16
AUG = 16


def params(mib):
    return pltpu.CompilerParams(vmem_limit_bytes=mib * 1024 * 1024)


def cost(us):
    return pl.CostEstimate(flops=int(us * 1.15e9), bytes_accessed=0, transcendentals=0)


def vmem():
    return pl.BlockSpec(memory_space=pltpu.VMEM)


def hbm():
    return pl.BlockSpec(memory_space=pl.ANY)


def smem():
    return pl.BlockSpec(memory_space=pltpu.SMEM)


def dot(a, b):
    return jnp.dot(a, b, preferred_element_type=F32)


def dot_nt(a, b):
    return lax.dot_general(a, b, (((1,), (1,)), ((), ())), preferred_element_type=F32)


def split(a):
    hi = a.astype(BF16)
    return hi, (a - hi.astype(F32)).astype(BF16)


def dot3(a, b, mul=dot):
    ah, al = a
    bh, bl = b
    return mul(ah, bh) + (mul(ah, bl) + mul(al, bh))


def start(copies):
    for copy in copies:
        copy.start()


def wait(copies):
    for copy in copies:
        copy.wait()


def slot_hot(order_ref):
    patches = order_ref.shape[1]
    ids = lax.broadcasted_iota(jnp.int32, (patches, patches), 0)
    return (ids == order_ref[...]).astype(F32)


def row_permutation(slots, members, gather):
    size = slots * members * gather
    target = lax.broadcasted_iota(jnp.int32, (size, size), 0)
    per = gather * members
    origin = lax.rem(target, per) * slots + lax.div(target, per)
    return (origin == lax.broadcasted_iota(jnp.int32, (size, size), 1)).astype(BF16)


def send_kernel(first, order_ref, x_ref, out_ref, x_buf, out_buf, x_sem, out_sem):
    fields, members, patches, cols = x_buf.shape
    groups, rows = out_buf.shape[1], out_buf.shape[2]
    slots = rows // members
    loads = [
        pltpu.make_async_copy(x_ref.at[:, f], x_buf.at[f], x_sem.at[f]) for f in range(fields)
    ]
    stores = [
        pltpu.make_async_copy(out_buf.at[f], out_ref.at[:, f], out_sem.at[f])
        for f in range(fields)
    ]
    start(loads)
    hot = slot_hot(order_ref).T.reshape(groups, patches // groups, patches)
    hot = hot[:, first : first + slots].reshape(groups * slots, patches).astype(BF16)
    for f in range(fields):
        loads[f].wait()
        parts = [dot(hot, x_buf[f, m]).reshape(groups, slots, cols) for m in range(members)]
        out_buf[f] = jnp.concatenate(parts, axis=1).astype(BF16)
        stores[f].start()
    wait(stores)


def send(order, x, first, slots, groups):
    members, fields, patches, cols = x.shape
    return pl.pallas_call(
        functools.partial(send_kernel, first),
        in_specs=[vmem(), hbm()],
        out_specs=hbm(),
        out_shape=jax.ShapeDtypeStruct((groups, fields, members * slots, cols), BF16),
        scratch_shapes=[
            pltpu.VMEM((fields, members, patches, cols), BF16),
            pltpu.VMEM((fields, groups, members * slots, cols), BF16),
            pltpu.SemaphoreType.DMA((fields,)),
            pltpu.SemaphoreType.DMA((fields,)),
        ],
        compiler_params=params(58),
        cost_estimate=cost(5),
        name="send_permute",
    )(order, x)


def tile_range(base, count, lev):
    return lax.div(base - lev + 3, 4), lax.div(base + count - lev + 3, 4)


def observe_kernel(first, counts_ref, lev_ref, recv_ref, op_ref, col_ref, *rest):
    x_ref, y_refs, scratch = rest[-16], rest[-15:-11], rest[-11:]
    recv_buf, x_buf, op_buf, col_buf, mean_ref, y_buf, recv_sem, x_sem, op_sem, col_sem, y_sem = scratch
    fields, groups, rows, cols = recv_buf.shape
    slots, members = x_buf.shape[1], x_buf.shape[2]
    members_local = rows // slots
    gather = 256 // rows
    part = members_local * gather
    loads = [
        pltpu.make_async_copy(recv_ref.at[:, f], recv_buf.at[f], recv_sem.at[f])
        for f in range(fields)
    ]
    stores = [
        pltpu.make_async_copy(x_buf.at[f], x_ref.at[f], x_sem.at[f]) for f in range(fields)
    ]
    small = [
        pltpu.make_async_copy(op_ref, op_buf, op_sem),
        pltpu.make_async_copy(col_ref, col_buf, col_sem),
    ]
    start(loads)
    start(small)
    perm = row_permutation(slots, members_local, gather)
    mean_ref[...] = jnp.zeros_like(mean_ref)
    for f in range(fields):
        loads[f].wait()
        for b in range(groups // gather):
            block = recv_buf[f, b * gather : (b + 1) * gather].reshape(gather * rows, cols)
            moved = dot(perm, block).astype(BF16).reshape(slots, part, cols)
            x_buf[f, :, b * part : (b + 1) * part, :] = moved
        stores[f].start()
    wait(small)

    begin = jnp.int32(0)
    for s in range(first):
        begin = begin + counts_ref[s]
    column_ids = lax.broadcasted_iota(jnp.int32, (cols, TILE), 0)

    def table_of(row):
        hit = (column_ids == col_buf[pl.ds(row, 1), :]).astype(BF16)
        weights = op_buf[row]
        return jnp.concatenate(
            [hit * weights[f : f + 1, :].astype(BF16) for f in range(fields)], axis=0
        )

    def store(local, y, mean):
        offset = lax.rem(local + 4 - lev_ref[0], 4)
        place = lax.div(local, 4)
        mean_ref[offset, pl.ds(place, 1), :] = mean
        y_buf[offset, pl.ds(pl.multiple_of(place * members, members), members), :] = (
            y - mean
        ).astype(BF16)

    def slot_step(s, base):
        count = counts_ref[first + s]

        def pair_step(i, carry):
            one = base + 2 * i
            two = jnp.minimum(one + 1, base + count - 1)
            table = jnp.concatenate([table_of(begin + one), table_of(begin + two)], axis=1)
            x = jnp.concatenate([x_buf[f, s] for f in range(fields)], axis=1)
            y = dot(x, table)
            mean = jnp.mean(y, axis=0, keepdims=True)
            store(one, y[:, :TILE], mean[:, :TILE])
            store(two, y[:, TILE:], mean[:, TILE:])
            return carry

        lax.fori_loop(0, lax.div(count + 1, 2), pair_step, 0)
        return base + count

    lax.fori_loop(0, slots, slot_step, jnp.int32(0))
    for d in range(4):
        mean = mean_ref[d]
        hi = mean.astype(BF16)
        mid = (mean - hi.astype(F32)).astype(BF16)
        low = (mean - hi.astype(F32) - mid.astype(F32)).astype(BF16)
        y_buf[d, y_buf.shape[1] - 48 :, :] = jnp.concatenate([hi, mid, low], axis=0)
    outs = [pltpu.make_async_copy(y_buf.at[d], y_refs[d], y_sem.at[d]) for d in range(4)]
    start(outs)
    wait(outs)
    wait(stores)


def observe(counts, lev, recv, op, col, first, slots, tiles, us, after):
    groups, fields, rows, cols = recv.shape
    members = groups * rows // slots
    length = tiles // 4 * members + 48
    return pl.pallas_call(
        functools.partial(observe_kernel, first),
        in_specs=[smem(), smem(), hbm(), hbm(), hbm()] + [hbm() for _ in after],
        out_specs=[hbm()] * 5,
        out_shape=[jax.ShapeDtypeStruct((fields, slots, members, cols), BF16)]
        + [jax.ShapeDtypeStruct((length, TILE), BF16)] * 4,
        scratch_shapes=[
            pltpu.VMEM((fields, groups, rows, cols), BF16),
            pltpu.VMEM((fields, slots, members, cols), BF16),
            pltpu.VMEM(op.shape, F32),
            pltpu.VMEM(col.shape, jnp.int32),
            pltpu.VMEM((4, 16, TILE), F32),
            pltpu.VMEM((4, length, TILE), BF16),
            pltpu.SemaphoreType.DMA((fields,)),
            pltpu.SemaphoreType.DMA((fields,)),
            pltpu.SemaphoreType.DMA,
            pltpu.SemaphoreType.DMA,
            pltpu.SemaphoreType.DMA((4,)),
        ],
        compiler_params=params(58),
        cost_estimate=cost(us),
        name="observe",
    )(counts, lev, recv, op, col, *after)


def gram_kernel(first, counts_ref, lev_ref, y0, y1, y2, y3, value_ref, weight_ref, *rest):
    out_refs, mean_ref = rest[-5:-1], rest[-1]
    per, _, members = out_refs[0].shape
    lev = lev_ref[0]
    start = jnp.int32(0)
    for s in range(first):
        start = start + counts_ref[s]
    tail = y0.shape[0] - 48
    total = (y0[tail:].astype(F32) + y1[tail:].astype(F32)) + (
        y2[tail:].astype(F32) + y3[tail:].astype(F32)
    )
    mean_ref[...] = total[0:16] + (total[16:32] + total[32:48])
    for d, out_ref in enumerate(out_refs):
        out_ref[...] = jnp.zeros_like(out_ref)
        owned = lax.rem(lev + d, 4) * per
        base = lax.fori_loop(0, owned, lambda s, b: b + counts_ref[first + s], jnp.int32(0))
        for s in range(per):
            count = counts_ref[first + owned + s]

            def tile_step(i, carry, s=s, out_ref=out_ref):
                row = start + 4 * i + lev
                rows = pl.ds(pl.multiple_of(i * members, members), members)
                pert = (y0[rows, :].astype(F32) + y1[rows, :].astype(F32)) + (
                    y2[rows, :].astype(F32) + y3[rows, :].astype(F32)
                )
                mean = mean_ref[pl.ds(i, 1), :]
                weight = weight_ref[pl.ds(row, 1), :]
                depart = value_ref[pl.ds(row, 1), :] - mean
                aug = jnp.concatenate([pert, depart, jnp.zeros((AUG - 1, TILE), F32)], axis=0)
                out_ref[s] += dot3(split(aug * weight), split(pert), dot_nt)
                return carry

            low, high = tile_range(base, count, lev)
            lax.fori_loop(low, high, tile_step, 0)
            base = base + count


def partial_gram(counts, lev, ys, value, weight, first, slots, members, us, after):
    return pl.pallas_call(
        functools.partial(gram_kernel, first),
        in_specs=[smem(), smem()] + [vmem()] * 6 + [hbm() for _ in after],
        out_specs=[vmem()] * 4,
        out_shape=[jax.ShapeDtypeStruct((slots // 4, members + AUG, members), F32)] * 4,
        scratch_shapes=[pltpu.VMEM((16, TILE), F32)],
        compiler_params=params(24),
        cost_estimate=cost(us),
        name="gram",
    )(counts, lev, *ys, value, weight, *after)


def solve_kernel(g0, g1, g2, g3, *rest):
    out_ref = rest[-1]
    slots, members = out_ref.shape[0], out_ref.shape[1]
    row = lax.broadcasted_iota(jnp.int32, (members, members), 0)
    eye = (row == lax.broadcasted_iota(jnp.int32, (members, members), 1)).astype(F32)
    uppers, lowers, scales, sides = [], [], [], []
    for s in range(slots):
        total = (g0[s] + g1[s]) + (g2[s] + g3[s])
        system = total[0:members] + (members - 1.0) * eye
        square = jnp.sum(jnp.sum(system * system, axis=1, keepdims=True), axis=0, keepdims=True)
        scale = jnp.sqrt(square)
        uppers.append(system / scale)
        lowers.append(eye)
        scales.append(scale)
        sides.append(total[members : members + 8])

    for step in range(ITERS):
        for s in range(slots):
            upper = split(uppers[s])
            if step == 0:
                middle = 1.5 * eye - 0.5 * uppers[s]
                lowers[s] = middle
                uppers[s] = dot3(upper, split(middle))
                continue
            lower = split(lowers[s])
            middle = split(1.5 * eye - 0.5 * dot3(lower, upper))
            lowers[s] = dot3(middle, lower)
            if step < ITERS - 1:
                uppers[s] = dot3(upper, middle)
    for s in range(slots):
        root = lowers[s] / jnp.sqrt(scales[s])
        parts = split(root)
        inner = dot3(split(sides[s]), parts, dot_nt)
        wmean = dot3(split(inner), parts, dot_nt)[0:1]
        out_ref[s] = (jnp.sqrt(jnp.float32(members - 1.0)) * root + wmean).astype(BF16)


def solve(gs, us, after):
    slots, _, members = gs[0].shape
    return pl.pallas_call(
        solve_kernel,
        in_specs=[vmem()] * 4 + [hbm() for _ in after],
        out_specs=vmem(),
        out_shape=jax.ShapeDtypeStruct((slots, members, members), BF16),
        compiler_params=params(24),
        cost_estimate=cost(us),
        name="newton_schulz",
    )(*gs, *after)


def apply_kernel(lev_ref, w0, w1, w2, w3, x_ref, *rest):
    out_ref, x_buf, mixed_ref, out_buf, x_sem, out_sem = rest[-6:]
    fields, slots, members, cols = x_buf.shape
    groups, rows = out_buf.shape[1], out_buf.shape[2]
    members_local = rows // slots
    gather = 256 // rows
    part = members_local * gather
    per = slots // 4
    loads = [
        pltpu.make_async_copy(x_ref.at[f], x_buf.at[f], x_sem.at[f]) for f in range(fields)
    ]
    stores = [
        pltpu.make_async_copy(out_buf.at[f], out_ref.at[:, f], out_sem.at[f])
        for f in range(fields)
    ]
    start(loads)
    perm = row_permutation(slots, members_local, gather).astype(F32).T.astype(BF16)
    for f in range(fields):
        loads[f].wait()
        for d, w_ref in enumerate((w0, w1, w2, w3)):
            owned = lax.rem(lev_ref[0] + 4 - d, 4) * per
            for s in range(per):
                x = x_buf[f, owned + s].astype(F32)
                mean = jnp.mean(x, axis=0, keepdims=True)
                mixed = dot(w_ref[s], (x - mean).astype(BF16))
                mixed_ref[owned + s] = (mean + mixed).astype(BF16)
        for b in range(groups // gather):
            block = mixed_ref[:, b * part : (b + 1) * part, :].reshape(slots * part, cols)
            moved = dot(perm, block).astype(BF16).reshape(gather, rows, cols)
            out_buf[f, b * gather : (b + 1) * gather] = moved
        stores[f].start()
    wait(stores)


def apply(lev, ws, x, groups, us, after):
    fields, slots, members, cols = x.shape
    rows = slots * members // groups
    return pl.pallas_call(
        apply_kernel,
        in_specs=[smem()] + [vmem()] * 4 + [hbm()] + [hbm() for _ in after],
        out_specs=hbm(),
        out_shape=jax.ShapeDtypeStruct((groups, fields, rows, cols), BF16),
        scratch_shapes=[
            pltpu.VMEM((fields, slots, members, cols), BF16),
            pltpu.VMEM((slots, members, cols), BF16),
            pltpu.VMEM((fields, groups, rows, cols), BF16),
            pltpu.SemaphoreType.DMA((fields,)),
            pltpu.SemaphoreType.DMA((fields,)),
        ],
        compiler_params=params(58),
        cost_estimate=cost(us),
        name="apply_weights",
    )(lev, *ws, x, *after)


def restore_kernel(order_ref, *refs):
    half = (len(refs) - 4) // 2
    recvs, out_ref, bufs = refs[:half], refs[half], refs[half + 1 : 2 * half + 1]
    out_buf, recv_sem, out_sem = refs[-3:]
    fields, members, patches, cols = out_buf.shape
    loads = [
        [
            pltpu.make_async_copy(r.at[:, f], b.at[f], recv_sem.at[f, c])
            for c, (r, b) in enumerate(zip(recvs, bufs))
        ]
        for f in range(fields)
    ]
    stores = [
        pltpu.make_async_copy(out_buf.at[f], out_ref.at[:, f], out_sem.at[f])
        for f in range(fields)
    ]
    for f in range(fields):
        start(loads[f])
    hot = slot_hot(order_ref).astype(BF16)
    for f in range(fields):
        wait(loads[f])
        blocks = [b[f].astype(F32) for b in bufs]
        for m in range(members):
            parts = []
            for block in blocks:
                slots = block.shape[1] // members
                parts.append(block[:, m * slots : (m + 1) * slots])
            stacked = jnp.concatenate(parts, axis=1).reshape(patches, cols).astype(BF16)
            out_buf[f, m] = dot(hot, stacked).astype(BF16)
        stores[f].start()
    wait(stores)


def restore(order, recvs, members):
    fields, cols = recvs[0].shape[1], recvs[0].shape[3]
    patches = order.shape[1]
    return pl.pallas_call(
        restore_kernel,
        in_specs=[vmem()] + [hbm()] * len(recvs),
        out_specs=hbm(),
        out_shape=jax.ShapeDtypeStruct((members, fields, patches, cols), BF16),
        scratch_shapes=[
            pltpu.VMEM((fields, r.shape[0], r.shape[2], cols), BF16) for r in recvs
        ]
        + [
            pltpu.VMEM((fields, members, patches, cols), BF16),
            pltpu.SemaphoreType.DMA((fields, len(recvs))),
            pltpu.SemaphoreType.DMA((fields,)),
        ],
        compiler_params=params(58),
        cost_estimate=cost(6),
        name="restore_order",
    )(order, *recvs)


def exchange(blocks):
    return [blocks[0]] + [
        lax.ppermute(blocks[d], "lev", [(i, (i + d) % 4) for i in range(4)]) for d in range(1, 4)
    ]


def body(background, patch_order, tile_counts, obs_column, obs_operator, obs_value, obs_weight):
    members_local, _, patches, fields, columns = background.shape
    slots_dev = tile_counts.shape[0]
    groups = patches // slots_dev
    tiles = obs_column.shape[0] // TILE
    level = lax.axis_index("lev")
    lev = jnp.reshape(level, (1,)).astype(jnp.int32)
    x = jnp.transpose(background[:, 0], (0, 2, 1, 3))
    order = patch_order.reshape(1, patches)
    col = obs_column.reshape(tiles, TILE)
    value = obs_value.reshape(tiles, TILE)
    weight = obs_weight.reshape(tiles, TILE)
    op = lax.dynamic_index_in_dim(obs_operator, level, 0, keepdims=False)
    op = jnp.transpose(op.reshape(fields, tiles, TILE), (1, 0, 2)).astype(F32)
    op = jnp.pad(op, ((0, 0), (0, 8 - fields), (0, 0)))

    gathered, firsts = [], []
    first = 0
    for slots in CHUNKS:
        if first > 0:
            order, op = lax.optimization_barrier((order, op))
        sent = send(order, x, first, slots, groups)
        gathered.append(lax.all_to_all(sent, "patch", split_axis=0, concat_axis=0, tiled=True))
        firsts.append(first)
        first += slots

    chunks = list(zip(CHUNKS, firsts, gathered))

    def see(c, us, after):
        slots, first, recv = chunks[c]
        room = tiles - (slots_dev - slots)
        x, *ys = observe(tile_counts, lev, recv, op, col, first, slots, room, us, after)
        return x, ys

    def weigh(c, ys, us, after):
        slots, first, _ = chunks[c]
        return partial_gram(tile_counts, lev, ys, value, weight, first, slots, members, us, after)

    def analyse(x, w, us, after):
        out = apply(lev, exchange([w] * 4), x, groups, us, after)
        return out, lax.all_to_all(out, "patch", split_axis=0, concat_axis=0, tiled=True)

    members = members_local * groups
    x0, ys0 = see(0, 200, [sent])
    gs0 = weigh(0, exchange(ys0), 1, [])
    x1, ys1 = see(1, 20, [gs0[0]])
    w0 = solve(exchange(gs0), 7, [ys1[0]])
    out0, back0 = analyse(x0, w0, 100, [])
    gs1 = weigh(1, exchange(ys1), 200, [out0])
    w1 = solve(exchange(gs1), 1, [])
    _, back1 = analyse(x1, w1, 1, [])
    backs = [back0, back1]

    result = restore(order, backs, members_local)
    return jnp.transpose(result, (0, 2, 1, 3))[:, None]


def solution(mesh):
    in_specs = (
        P("patch", "lev", None, None, None),
        P(),
        P("patch"),
        P("patch"),
        P(None, None, "patch"),
        P("patch"),
        P("patch"),
    )
    out_specs = P("patch", "lev", None, None, None)
    return jax.shard_map(body, mesh=mesh, in_specs=in_specs, out_specs=out_specs, check_vma=False)
```

```python
import functools

import jax
import jax.numpy as jnp
from jax import lax
from jax.experimental import pallas as pl
from jax.experimental.pallas import tpu as pltpu
from jax.sharding import PartitionSpec as P

TILE = 128
ITERS = 10
CHUNKS = (8, 8)
F32 = jnp.float32
BF16 = jnp.bfloat16
AUG = 16


def params(mib):
    return pltpu.CompilerParams(vmem_limit_bytes=mib * 1024 * 1024)


def cost(us):
    return pl.CostEstimate(flops=int(us * 1.15e9), bytes_accessed=0, transcendentals=0)


def vmem():
    return pl.BlockSpec(memory_space=pltpu.VMEM)


def hbm():
    return pl.BlockSpec(memory_space=pl.ANY)


def smem():
    return pl.BlockSpec(memory_space=pltpu.SMEM)


def dot(a, b):
    return jnp.dot(a, b, preferred_element_type=F32)


def dot_nt(a, b):
    return lax.dot_general(a, b, (((1,), (1,)), ((), ())), preferred_element_type=F32)


def split(a):
    hi = a.astype(BF16)
    return hi, (a - hi.astype(F32)).astype(BF16)


def dot3(a, b, mul=dot):
    ah, al = a
    bh, bl = b
    return mul(ah, bh) + (mul(ah, bl) + mul(al, bh))


def start(copies):
    for copy in copies:
        copy.start()


def wait(copies):
    for copy in copies:
        copy.wait()


def slot_hot(order_ref):
    patches = order_ref.shape[1]
    ids = lax.broadcasted_iota(jnp.int32, (patches, patches), 0)
    return (ids == order_ref[...]).astype(F32)


def row_permutation(slots, members, gather):
    size = slots * members * gather
    target = lax.broadcasted_iota(jnp.int32, (size, size), 0)
    per = gather * members
    origin = lax.rem(target, per) * slots + lax.div(target, per)
    return (origin == lax.broadcasted_iota(jnp.int32, (size, size), 1)).astype(BF16)


def send_kernel(first, order_ref, x_ref, out_ref, x_buf, out_buf, x_sem, out_sem):
    fields, members, patches, cols = x_buf.shape
    groups, rows = out_buf.shape[1], out_buf.shape[2]
    slots = rows // members
    loads = [
        pltpu.make_async_copy(x_ref.at[:, f], x_buf.at[f], x_sem.at[f]) for f in range(fields)
    ]
    stores = [
        pltpu.make_async_copy(out_buf.at[f], out_ref.at[:, f], out_sem.at[f])
        for f in range(fields)
    ]
    start(loads)
    hot = slot_hot(order_ref).T.reshape(groups, patches // groups, patches)
    hot = hot[:, first : first + slots].reshape(groups * slots, patches).astype(BF16)
    for f in range(fields):
        loads[f].wait()
        parts = [dot(hot, x_buf[f, m]).reshape(groups, slots, cols) for m in range(members)]
        out_buf[f] = jnp.concatenate(parts, axis=1).astype(BF16)
        stores[f].start()
    wait(stores)


def send(order, x, first, slots, groups):
    members, fields, patches, cols = x.shape
    return pl.pallas_call(
        functools.partial(send_kernel, first),
        in_specs=[vmem(), hbm()],
        out_specs=hbm(),
        out_shape=jax.ShapeDtypeStruct((groups, fields, members * slots, cols), BF16),
        scratch_shapes=[
            pltpu.VMEM((fields, members, patches, cols), BF16),
            pltpu.VMEM((fields, groups, members * slots, cols), BF16),
            pltpu.SemaphoreType.DMA((fields,)),
            pltpu.SemaphoreType.DMA((fields,)),
        ],
        compiler_params=params(62),
        cost_estimate=cost(5),
        name="send_permute",
    )(order, x)


def tile_range(base, count, lev):
    return lax.div(base - lev + 3, 4), lax.div(base + count - lev + 3, 4)


def observe_kernel(first, counts_ref, lev_ref, recv_ref, op_ref, col_ref, *rest):
    x_ref, y_refs, scratch = rest[-16], rest[-15:-11], rest[-11:]
    recv_buf, x_buf, op_buf, col_buf, mean_ref, y_buf, recv_sem, x_sem, op_sem, col_sem, y_sem = scratch
    fields, groups, rows, cols = recv_buf.shape
    slots, members = x_buf.shape[1], x_buf.shape[2]
    members_local = rows // slots
    gather = 256 // rows
    part = members_local * gather
    loads = [
        pltpu.make_async_copy(recv_ref.at[:, f], recv_buf.at[f], recv_sem.at[f])
        for f in range(fields)
    ]
    stores = [
        pltpu.make_async_copy(x_buf.at[f], x_ref.at[f], x_sem.at[f]) for f in range(fields)
    ]
    small = [
        pltpu.make_async_copy(op_ref, op_buf, op_sem),
        pltpu.make_async_copy(col_ref, col_buf, col_sem),
    ]
    start(loads)
    start(small)
    perm = row_permutation(slots, members_local, gather)
    mean_ref[...] = jnp.zeros_like(mean_ref)
    for f in range(fields):
        loads[f].wait()
        block = recv_buf[f].astype(F32).reshape(members, slots, cols)
        x_buf[f] = jnp.transpose(block, (1, 0, 2)).astype(BF16)
        stores[f].start()
    wait(small)

    begin = jnp.int32(0)
    for s in range(first):
        begin = begin + counts_ref[s]
    column_ids = lax.broadcasted_iota(jnp.int32, (cols, TILE), 0)

    def table_of(row):
        hit = (column_ids == col_buf[pl.ds(row, 1), :]).astype(BF16)
        weights = op_buf[row]
        return jnp.concatenate(
            [hit * weights[f : f + 1, :].astype(BF16) for f in range(fields)], axis=0
        )

    def store(local, y, mean):
        offset = lax.rem(local + 4 - lev_ref[0], 4)
        place = lax.div(local, 4)
        mean_ref[offset, pl.ds(place, 1), :] = mean
        y_buf[offset, pl.ds(pl.multiple_of(place * members, members), members), :] = (
            y - mean
        ).astype(BF16)

    def slot_step(s, base):
        count = counts_ref[first + s]

        def observed(one, two):
            table = jnp.concatenate([table_of(begin + one), table_of(begin + two)], axis=1)
            x = jnp.concatenate([x_buf[f, s] for f in range(fields)], axis=1)
            y = dot(x, table)
            return y, jnp.mean(y, axis=0, keepdims=True)

        def store_both(one, two, result):
            y, mean = result
            store(one, y[:, :TILE], mean[:, :TILE])
            store(two, y[:, TILE:], mean[:, TILE:])

        def quad_step(i, carry):
            one = base + 4 * i
            results = observed(one, one + 1), observed(one + 2, one + 3)
            store_both(one, one + 1, results[0])
            store_both(one + 2, one + 3, results[1])
            return carry

        def oct_step(i, carry):
            ones = [base + 8 * i + 2 * n for n in range(4)]
            results = [observed(one, one + 1) for one in ones]
            for one, result in zip(ones, results):
                store_both(one, one + 1, result)
            return carry

        def pair_step(i, carry):
            one = base + 2 * i
            two = jnp.minimum(one + 1, base + count - 1)
            store_both(one, two, observed(one, two))
            return carry

        octs, quads = lax.div(count, 8), lax.div(count, 4)
        lax.fori_loop(0, octs, oct_step, 0)
        lax.fori_loop(2 * octs, quads, quad_step, 0)
        lax.fori_loop(2 * quads, lax.div(count + 1, 2), pair_step, 0)
        return base + count

    lax.fori_loop(0, slots, slot_step, jnp.int32(0))
    for d in range(4):
        mean = mean_ref[d]
        hi = mean.astype(BF16)
        mid = (mean - hi.astype(F32)).astype(BF16)
        low = (mean - hi.astype(F32) - mid.astype(F32)).astype(BF16)
        y_buf[d, y_buf.shape[1] - 48 :, :] = jnp.concatenate([hi, mid, low], axis=0)
    outs = [pltpu.make_async_copy(y_buf.at[d], y_refs[d], y_sem.at[d]) for d in range(4)]
    start(outs)
    wait(outs)
    wait(stores)


def observe(counts, lev, recv, op, col, first, slots, tiles, us, mib, after):
    groups, fields, rows, cols = recv.shape
    members = groups * rows // slots
    length = tiles // 4 * members + 48
    return pl.pallas_call(
        functools.partial(observe_kernel, first),
        in_specs=[smem(), smem(), hbm(), hbm(), hbm()] + [hbm() for _ in after],
        out_specs=[hbm()] * 5,
        out_shape=[jax.ShapeDtypeStruct((fields, slots, members, cols), BF16)]
        + [jax.ShapeDtypeStruct((length, TILE), BF16)] * 4,
        scratch_shapes=[
            pltpu.VMEM((fields, groups, rows, cols), BF16),
            pltpu.VMEM((fields, slots, members, cols), BF16),
            pltpu.VMEM(op.shape, F32),
            pltpu.VMEM(col.shape, jnp.int32),
            pltpu.VMEM((4, 16, TILE), F32),
            pltpu.VMEM((4, length, TILE), BF16),
            pltpu.SemaphoreType.DMA((fields,)),
            pltpu.SemaphoreType.DMA((fields,)),
            pltpu.SemaphoreType.DMA,
            pltpu.SemaphoreType.DMA,
            pltpu.SemaphoreType.DMA((4,)),
        ],
        compiler_params=params(mib),
        cost_estimate=cost(us),
        name="observe",
    )(counts, lev, recv, op, col, *after)


def gram_kernel(first, counts_ref, lev_ref, y0, y1, y2, y3, value_ref, weight_ref, *rest):
    out_refs, mean_ref = rest[-5:-1], rest[-1]
    per, _, members = out_refs[0].shape
    lev = lev_ref[0]
    start = jnp.int32(0)
    for s in range(first):
        start = start + counts_ref[s]
    tail = y0.shape[0] - 48
    total = (y0[tail:].astype(F32) + y1[tail:].astype(F32)) + (
        y2[tail:].astype(F32) + y3[tail:].astype(F32)
    )
    mean_ref[...] = total[0:16] + (total[16:32] + total[32:48])
    for d, out_ref in enumerate(out_refs):
        out_ref[...] = jnp.zeros_like(out_ref)
        owned = lax.rem(lev + d, 4) * per
        base = lax.fori_loop(0, owned, lambda s, b: b + counts_ref[first + s], jnp.int32(0))
        for s in range(per):
            count = counts_ref[first + owned + s]

            def tile_step(i, carry, s=s, out_ref=out_ref):
                row = start + 4 * i + lev
                rows = pl.ds(pl.multiple_of(i * members, members), members)
                pert = (y0[rows, :].astype(F32) + y1[rows, :].astype(F32)) + (
                    y2[rows, :].astype(F32) + y3[rows, :].astype(F32)
                )
                mean = mean_ref[pl.ds(i, 1), :]
                weight = weight_ref[pl.ds(row, 1), :]
                depart = value_ref[pl.ds(row, 1), :] - mean
                aug = jnp.concatenate([pert, depart, jnp.zeros((AUG - 1, TILE), F32)], axis=0)
                out_ref[s] += dot3(split(aug * weight), split(pert), dot_nt)
                return carry

            low, high = tile_range(base, count, lev)
            lax.fori_loop(low, high, tile_step, 0)
            base = base + count


def partial_gram(counts, lev, ys, value, weight, first, slots, members, us, after):
    return pl.pallas_call(
        functools.partial(gram_kernel, first),
        in_specs=[smem(), smem()] + [vmem()] * 6 + [hbm() for _ in after],
        out_specs=[vmem()] * 4,
        out_shape=[jax.ShapeDtypeStruct((slots // 4, members + AUG, members), F32)] * 4,
        scratch_shapes=[pltpu.VMEM((16, TILE), F32)],
        compiler_params=params(24),
        cost_estimate=cost(us),
        name="gram",
    )(counts, lev, *ys, value, weight, *after)


def solve_kernel(g0, g1, g2, g3, *rest):
    out_ref = rest[-1]
    slots, members = out_ref.shape[0], out_ref.shape[1]
    row = lax.broadcasted_iota(jnp.int32, (members, members), 0)
    eye = (row == lax.broadcasted_iota(jnp.int32, (members, members), 1)).astype(F32)
    uppers, lowers, scales, sides = [], [], [], []
    for s in range(slots):
        total = (g0[s] + g1[s]) + (g2[s] + g3[s])
        system = total[0:members] + (members - 1.0) * eye
        square = jnp.sum(jnp.sum(system * system, axis=1, keepdims=True), axis=0, keepdims=True)
        scale = jnp.sqrt(square)
        uppers.append(system / scale)
        lowers.append(eye)
        scales.append(scale)
        sides.append(total[members : members + 8])

    for step in range(ITERS):
        for s in range(slots):
            upper = split(uppers[s])
            if step == 0:
                middle = 1.5 * eye - 0.5 * uppers[s]
                lowers[s] = middle
                uppers[s] = dot3(upper, split(middle))
                continue
            lower = split(lowers[s])
            middle = split(1.5 * eye - 0.5 * dot3(lower, upper))
            lowers[s] = dot3(middle, lower)
            if step < ITERS - 1:
                uppers[s] = dot3(upper, middle)
    for s in range(slots):
        root = lowers[s] / jnp.sqrt(scales[s])
        parts = split(root)
        inner = dot3(split(sides[s]), parts, dot_nt)
        wmean = dot3(split(inner), parts, dot_nt)[0:1]
        out_ref[s] = (jnp.sqrt(jnp.float32(members - 1.0)) * root + wmean).astype(BF16)


def solve(gs, us, after):
    slots, _, members = gs[0].shape
    return pl.pallas_call(
        solve_kernel,
        in_specs=[vmem()] * 4 + [hbm() for _ in after],
        out_specs=vmem(),
        out_shape=jax.ShapeDtypeStruct((slots, members, members), BF16),
        compiler_params=params(24),
        cost_estimate=cost(us),
        name="newton_schulz",
    )(*gs, *after)


def apply_kernel(lev_ref, w0, w1, w2, w3, x_ref, *rest):
    out_ref, x_buf, mixed_ref, out_buf, x_sem, out_sem = rest[-6:]
    fields, slots, members, cols = x_buf.shape
    groups, rows = out_buf.shape[1], out_buf.shape[2]
    members_local = rows // slots
    gather = 256 // rows
    part = members_local * gather
    per = slots // 4
    loads = [
        pltpu.make_async_copy(x_ref.at[f], x_buf.at[f], x_sem.at[f]) for f in range(fields)
    ]
    stores = [
        pltpu.make_async_copy(out_buf.at[f], out_ref.at[:, f], out_sem.at[f])
        for f in range(fields)
    ]
    start(loads)
    perm = row_permutation(slots, members_local, gather).astype(F32).T.astype(BF16)
    for f in range(fields):
        loads[f].wait()
        for d, w_ref in enumerate((w0, w1, w2, w3)):
            owned = lax.rem(lev_ref[0] + 4 - d, 4) * per
            for s in range(per):
                x = x_buf[f, owned + s].astype(F32)
                mean = jnp.mean(x, axis=0, keepdims=True)
                mixed = dot(w_ref[s], (x - mean).astype(BF16))
                mixed_ref[owned + s] = mean + mixed
        moved = jnp.transpose(mixed_ref[...], (1, 0, 2)).reshape(groups, rows, cols)
        out_buf[f] = moved.astype(BF16)
        stores[f].start()
    wait(stores)


def apply(lev, ws, x, groups, us, mib, after):
    fields, slots, members, cols = x.shape
    rows = slots * members // groups
    return pl.pallas_call(
        apply_kernel,
        in_specs=[smem()] + [vmem()] * 4 + [hbm()] + [hbm() for _ in after],
        out_specs=hbm(),
        out_shape=jax.ShapeDtypeStruct((groups, fields, rows, cols), BF16),
        scratch_shapes=[
            pltpu.VMEM((fields, slots, members, cols), BF16),
            pltpu.VMEM((slots, members, cols), F32),
            pltpu.VMEM((fields, groups, rows, cols), BF16),
            pltpu.SemaphoreType.DMA((fields,)),
            pltpu.SemaphoreType.DMA((fields,)),
        ],
        compiler_params=params(mib),
        cost_estimate=cost(us),
        name="apply_weights",
    )(lev, *ws, x, *after)


def restore_kernel(order_ref, *refs):
    half = (len(refs) - 4) // 2
    recvs, out_ref, bufs = refs[:half], refs[half], refs[half + 1 : 2 * half + 1]
    out_buf, recv_sem, out_sem = refs[-3:]
    fields, members, patches, cols = out_buf.shape
    loads = [
        [
            pltpu.make_async_copy(r.at[:, f], b.at[f], recv_sem.at[f, c])
            for c, (r, b) in enumerate(zip(recvs, bufs))
        ]
        for f in range(fields)
    ]
    stores = [
        pltpu.make_async_copy(out_buf.at[f], out_ref.at[:, f], out_sem.at[f])
        for f in range(fields)
    ]
    for f in range(fields):
        start(loads[f])
    hot = slot_hot(order_ref).astype(BF16)
    for f in range(fields):
        wait(loads[f])
        blocks = [b[f].astype(F32) for b in bufs]
        for m in range(members):
            parts = []
            for block in blocks:
                slots = block.shape[1] // members
                parts.append(block[:, m * slots : (m + 1) * slots])
            stacked = jnp.concatenate(parts, axis=1).reshape(patches, cols).astype(BF16)
            out_buf[f, m] = dot(hot, stacked).astype(BF16)
        stores[f].start()
    wait(stores)


def restore(order, recvs, members):
    fields, cols = recvs[0].shape[1], recvs[0].shape[3]
    patches = order.shape[1]
    return pl.pallas_call(
        restore_kernel,
        in_specs=[vmem()] + [hbm()] * len(recvs),
        out_specs=hbm(),
        out_shape=jax.ShapeDtypeStruct((members, fields, patches, cols), BF16),
        scratch_shapes=[
            pltpu.VMEM((fields, r.shape[0], r.shape[2], cols), BF16) for r in recvs
        ]
        + [
            pltpu.VMEM((fields, members, patches, cols), BF16),
            pltpu.SemaphoreType.DMA((fields, len(recvs))),
            pltpu.SemaphoreType.DMA((fields,)),
        ],
        compiler_params=params(62),
        cost_estimate=cost(6),
        name="restore_order",
    )(order, *recvs)


def exchange(blocks):
    return [blocks[0]] + [
        lax.ppermute(blocks[d], "lev", [(i, (i + d) % 4) for i in range(4)]) for d in range(1, 4)
    ]


def body(background, patch_order, tile_counts, obs_column, obs_operator, obs_value, obs_weight):
    members_local, _, patches, fields, columns = background.shape
    slots_dev = tile_counts.shape[0]
    groups = patches // slots_dev
    tiles = obs_column.shape[0] // TILE
    level = lax.axis_index("lev")
    lev = jnp.reshape(level, (1,)).astype(jnp.int32)
    x = jnp.transpose(background[:, 0], (0, 2, 1, 3))
    order = patch_order.reshape(1, patches)
    col = obs_column.reshape(tiles, TILE)
    value = obs_value.reshape(tiles, TILE)
    weight = obs_weight.reshape(tiles, TILE)
    op = lax.dynamic_index_in_dim(obs_operator, level, 0, keepdims=False)
    op = jnp.transpose(op.reshape(fields, tiles, TILE), (1, 0, 2)).astype(F32)
    op = jnp.pad(op, ((0, 0), (0, 8 - fields), (0, 0)))

    gathered, firsts = [], []
    first = 0
    for slots in CHUNKS:
        if first > 0:
            order, op = lax.optimization_barrier((order, op))
        sent = send(order, x, first, slots, groups)
        gathered.append(lax.all_to_all(sent, "patch", split_axis=0, concat_axis=0, tiled=True))
        firsts.append(first)
        first += slots

    chunks = list(zip(CHUNKS, firsts, gathered))

    def see(c, us, after):
        slots, first, recv = chunks[c]
        room = tiles - (slots_dev - slots)
        x, *ys = observe(tile_counts, lev, recv, op, col, first, slots, room, us, (62, 62)[c], after)
        return x, ys

    def weigh(c, ys, us, after):
        slots, first, _ = chunks[c]
        return partial_gram(tile_counts, lev, ys, value, weight, first, slots, members, us, after)

    def analyse(x, w, us, mib, after):
        out = apply(lev, exchange([w] * 4), x, groups, us, mib, after)
        return out, lax.all_to_all(out, "patch", split_axis=0, concat_axis=0, tiled=True)

    members = members_local * groups
    x0, ys0 = see(0, 1, [sent])
    gs0 = weigh(0, exchange(ys0), 200, [])
    w0 = solve(exchange(gs0), 7, [])
    x1, ys1 = see(1, 20, [w0])
    out0, back0 = analyse(x0, w0, 100, 62, [ys1[0]])
    gs1 = weigh(1, exchange(ys1), 200, [out0])
    w1 = solve(exchange(gs1), 1, [])
    _, back1 = analyse(x1, w1, 1, 62, [])
    backs = [back0, back1]

    result = restore(order, backs, members_local)
    return jnp.transpose(result, (0, 2, 1, 3))[:, None]


def solution(mesh):
    in_specs = (
        P("patch", "lev", None, None, None),
        P(),
        P("patch"),
        P("patch"),
        P(None, None, "patch"),
        P("patch"),
        P("patch"),
    )
    out_specs = P("patch", "lev", None, None, None)
    return jax.shard_map(body, mesh=mesh, in_specs=in_specs, out_specs=out_specs, check_vma=False)
```

```python
import functools

import jax
import jax.numpy as jnp
from jax import lax
from jax.experimental import pallas as pl
from jax.experimental.pallas import tpu as pltpu
from jax.sharding import PartitionSpec as P

TILE = 128
ITERS = 10
CHUNKS = (8, 8)
F32 = jnp.float32
BF16 = jnp.bfloat16
AUG = 16
AHEAD = 3


def params(mib):
    return pltpu.CompilerParams(vmem_limit_bytes=mib * 1024 * 1024)


def cost(us):
    return pl.CostEstimate(flops=int(us * 1.15e9), bytes_accessed=0, transcendentals=0)


def vmem():
    return pl.BlockSpec(memory_space=pltpu.VMEM)


def hbm():
    return pl.BlockSpec(memory_space=pl.ANY)


def smem():
    return pl.BlockSpec(memory_space=pltpu.SMEM)


def dot(a, b):
    return jnp.dot(a, b, preferred_element_type=F32)


def dot_nt(a, b):
    return lax.dot_general(a, b, (((1,), (1,)), ((), ())), preferred_element_type=F32)


def split(a):
    hi = a.astype(BF16)
    return hi, (a - hi.astype(F32)).astype(BF16)


def dot3(a, b, mul=dot):
    ah, al = a
    bh, bl = b
    return mul(ah, bh) + (mul(ah, bl) + mul(al, bh))


def start(copies):
    for copy in copies:
        copy.start()


def wait(copies):
    for copy in copies:
        copy.wait()


def slot_hot(order_ref):
    patches = order_ref.shape[1]
    ids = lax.broadcasted_iota(jnp.int32, (patches, patches), 0)
    return (ids == order_ref[...]).astype(F32)


def send_kernel(first, order_ref, x_ref, out_ref, x_buf, out_buf, x_sem, out_sem):
    fields, members, patches, cols = x_buf.shape
    groups, rows = out_buf.shape[1], out_buf.shape[2]
    slots = rows // members
    loads = [
        pltpu.make_async_copy(x_ref.at[:, f], x_buf.at[f], x_sem.at[f]) for f in range(fields)
    ]
    stores = [
        pltpu.make_async_copy(out_buf.at[f], out_ref.at[:, f], out_sem.at[f])
        for f in range(fields)
    ]
    start(loads)
    hot = slot_hot(order_ref).T.reshape(groups, patches // groups, patches)
    hot = hot[:, first : first + slots].reshape(groups * slots, patches).astype(BF16)
    for f in range(fields):
        loads[f].wait()
        parts = [dot(hot, x_buf[f, m]).reshape(groups, slots, cols) for m in range(members)]
        out_buf[f] = jnp.concatenate(parts, axis=1).astype(BF16)
        stores[f].start()
    wait(stores)


def send(order, x, first, slots, groups):
    members, fields, patches, cols = x.shape
    return pl.pallas_call(
        functools.partial(send_kernel, first),
        in_specs=[vmem(), hbm()],
        out_specs=hbm(),
        out_shape=jax.ShapeDtypeStruct((groups, fields, members * slots, cols), BF16),
        scratch_shapes=[
            pltpu.VMEM((fields, members, patches, cols), BF16),
            pltpu.VMEM((fields, groups, members * slots, cols), BF16),
            pltpu.SemaphoreType.DMA((fields,)),
            pltpu.SemaphoreType.DMA((fields,)),
        ],
        compiler_params=params(62),
        cost_estimate=cost(5),
        name="send_permute",
    )(order, x)


def tile_range(base, count, lev):
    return lax.div(base - lev + 3, 4), lax.div(base + count - lev + 3, 4)


def observe_kernel(first, counts_ref, lev_ref, recv_ref, op_ref, col_ref, *rest):
    x_ref, y_refs, scratch = rest[-16], rest[-15:-11], rest[-11:]
    recv_buf, x_buf, op_buf, col_buf, mean_ref, y_buf, recv_sem, x_sem, op_sem, col_sem, y_sem = scratch
    fields, groups, rows, cols = recv_buf.shape
    slots, members = x_buf.shape[1], x_buf.shape[2]
    loads = [
        pltpu.make_async_copy(recv_ref.at[:, f], recv_buf.at[f], recv_sem.at[f])
        for f in range(fields)
    ]
    stores = [
        pltpu.make_async_copy(x_buf.at[f], x_ref.at[f], x_sem.at[f]) for f in range(fields)
    ]
    small = [
        pltpu.make_async_copy(op_ref, op_buf, op_sem),
        pltpu.make_async_copy(col_ref, col_buf, col_sem),
    ]
    start(loads)
    start(small)
    mean_ref[...] = jnp.zeros_like(mean_ref)
    for f in range(fields):
        loads[f].wait()
        block = recv_buf[f].astype(F32).reshape(members, slots, cols)
        x_buf[f] = jnp.transpose(block, (1, 0, 2)).astype(BF16)
        stores[f].start()
    wait(small)

    begin = jnp.int32(0)
    for s in range(first):
        begin = begin + counts_ref[s]
    column_ids = lax.broadcasted_iota(jnp.int32, (cols, TILE), 0)

    def table_of(row):
        hit = (column_ids == col_buf[pl.ds(row, 1), :]).astype(BF16)
        weights = op_buf[row]
        return jnp.concatenate(
            [hit * weights[f : f + 1, :].astype(BF16) for f in range(fields)], axis=0
        )

    def store(local, y, mean):
        offset = lax.rem(local + 4 - lev_ref[0], 4)
        place = lax.div(local, 4)
        mean_ref[offset, pl.ds(place, 1), :] = mean
        y_buf[offset, pl.ds(pl.multiple_of(place * members, members), members), :] = (
            y - mean
        ).astype(BF16)

    def slot_step(s, base):
        count = counts_ref[first + s]

        def observed(one, two):
            table = jnp.concatenate([table_of(begin + one), table_of(begin + two)], axis=1)
            x = jnp.concatenate([x_buf[f, s] for f in range(fields)], axis=1)
            y = dot(x, table)
            return y, jnp.mean(y, axis=0, keepdims=True)

        def store_both(one, two, result):
            y, mean = result
            store(one, y[:, :TILE], mean[:, :TILE])
            store(two, y[:, TILE:], mean[:, TILE:])

        def quad_step(i, carry):
            one = base + 4 * i
            results = observed(one, one + 1), observed(one + 2, one + 3)
            store_both(one, one + 1, results[0])
            store_both(one + 2, one + 3, results[1])
            return carry

        def oct_step(i, carry):
            ones = [base + 8 * i + 2 * n for n in range(4)]
            results = [observed(one, one + 1) for one in ones]
            for one, result in zip(ones, results):
                store_both(one, one + 1, result)
            return carry

        def pair_step(i, carry):
            one = base + 2 * i
            two = jnp.minimum(one + 1, base + count - 1)
            store_both(one, two, observed(one, two))
            return carry

        octs, quads = lax.div(count, 8), lax.div(count, 4)
        lax.fori_loop(0, octs, oct_step, 0)
        lax.fori_loop(2 * octs, quads, quad_step, 0)
        lax.fori_loop(2 * quads, lax.div(count + 1, 2), pair_step, 0)
        return base + count

    lax.fori_loop(0, slots, slot_step, jnp.int32(0))
    for d in range(4):
        mean = mean_ref[d]
        hi = mean.astype(BF16)
        mid = (mean - hi.astype(F32)).astype(BF16)
        low = (mean - hi.astype(F32) - mid.astype(F32)).astype(BF16)
        y_buf[d, y_buf.shape[1] - 48 :, :] = jnp.concatenate([hi, mid, low], axis=0)
    outs = [pltpu.make_async_copy(y_buf.at[d], y_refs[d], y_sem.at[d]) for d in range(4)]
    start(outs)
    wait(outs)
    wait(stores)


def observe(counts, lev, recv, op, col, first, slots, tiles, us, mib, after):
    groups, fields, rows, cols = recv.shape
    members = groups * rows // slots
    length = tiles // 4 * members + 48
    return pl.pallas_call(
        functools.partial(observe_kernel, first),
        in_specs=[smem(), smem(), hbm(), hbm(), hbm()] + [hbm() for _ in after],
        out_specs=[hbm()] * 5,
        out_shape=[jax.ShapeDtypeStruct((fields, slots, members, cols), BF16)]
        + [jax.ShapeDtypeStruct((length, TILE), BF16)] * 4,
        scratch_shapes=[
            pltpu.VMEM((fields, groups, rows, cols), BF16),
            pltpu.VMEM((fields, slots, members, cols), BF16),
            pltpu.VMEM(op.shape, F32),
            pltpu.VMEM(col.shape, jnp.int32),
            pltpu.VMEM((4, 16, TILE), F32),
            pltpu.VMEM((4, length, TILE), BF16),
            pltpu.SemaphoreType.DMA((fields,)),
            pltpu.SemaphoreType.DMA((fields,)),
            pltpu.SemaphoreType.DMA,
            pltpu.SemaphoreType.DMA,
            pltpu.SemaphoreType.DMA((4,)),
        ],
        compiler_params=params(mib),
        cost_estimate=cost(us),
        name="observe",
    )(counts, lev, recv, op, col, *after)


def pack_rows(a):
    half = a.shape[1] // 2
    quarter = half // 2
    left = lax.broadcasted_iota(jnp.int32, (quarter, 2 * half), 1) < half
    corner = jnp.where(left, a[:quarter], pltpu.roll(a[quarter:half], half, 1))
    return jnp.concatenate([corner, a[half : 2 * half + 8]], axis=0)


def unpack_rows(a):
    half = a.shape[1] // 2
    quarter = half // 2
    top = jnp.concatenate([a[:quarter], pltpu.roll(a[:quarter], half, 1)], axis=0)
    lower = jnp.concatenate([top, a[quarter : quarter + half]], axis=0)
    row = lax.broadcasted_iota(jnp.int32, lower.shape, 0)
    col = lax.broadcasted_iota(jnp.int32, lower.shape, 1)
    matrix = jnp.where((row < half) & (col >= half), lower.T, lower)
    return matrix, a[quarter + half :]


def gram_kernel(first, counts_ref, lev_ref, y0, y1, y2, y3, value_ref, weight_ref, *rest):
    out_refs, mean_ref, sum_ref = rest[-6:-2], rest[-2], rest[-1]
    per, _, members = out_refs[0].shape
    lev = lev_ref[0]
    start = jnp.int32(0)
    for s in range(first):
        start = start + counts_ref[s]
    tail = y0.shape[0] - 48
    total = (y0[tail:].astype(F32) + y1[tail:].astype(F32)) + (
        y2[tail:].astype(F32) + y3[tail:].astype(F32)
    )
    mean_ref[...] = total[0:16] + (total[16:32] + total[32:48])
    for d, out_ref in enumerate(out_refs):
        owned = lax.rem(lev + d, 4) * per
        base = lax.fori_loop(0, owned, lambda s, b: b + counts_ref[first + s], jnp.int32(0))
        for s in range(per):
            count = counts_ref[first + owned + s]
            sum_ref[...] = jnp.zeros_like(sum_ref)

            def tile_step(i, carry):
                row = start + 4 * i + lev
                rows = pl.ds(pl.multiple_of(i * members, members), members)
                pert = (y0[rows, :].astype(F32) + y1[rows, :].astype(F32)) + (
                    y2[rows, :].astype(F32) + y3[rows, :].astype(F32)
                )
                mean = mean_ref[pl.ds(i, 1), :]
                weight = weight_ref[pl.ds(row, 1), :]
                depart = value_ref[pl.ds(row, 1), :] - mean
                aug = jnp.concatenate([pert, depart, jnp.zeros((AUG - 1, TILE), F32)], axis=0)
                sum_ref[...] += dot3(split(aug * weight), split(pert), dot_nt)
                return carry

            low, high = tile_range(base, count, lev)
            lax.fori_loop(low, high, tile_step, 0)
            base = base + count
            out_ref[s] = pack_rows(sum_ref[...])


def partial_gram(counts, lev, ys, value, weight, first, slots, members, us, after):
    return pl.pallas_call(
        functools.partial(gram_kernel, first),
        in_specs=[smem(), smem()] + [vmem()] * 6 + [hbm() for _ in after],
        out_specs=[vmem()] * 4,
        out_shape=[jax.ShapeDtypeStruct((slots // 4, members * 3 // 4 + 8, members), F32)] * 4,
        scratch_shapes=[
            pltpu.VMEM((16, TILE), F32),
            pltpu.VMEM((members + AUG, members), F32),
        ],
        compiler_params=params(24),
        cost_estimate=cost(us),
        name="gram",
    )(counts, lev, *ys, value, weight, *after)


def solve_kernel(g0, g1, g2, g3, *rest):
    out_ref = rest[-1]
    slots, members = out_ref.shape[0], out_ref.shape[1]
    row = lax.broadcasted_iota(jnp.int32, (members, members), 0)
    eye = (row == lax.broadcasted_iota(jnp.int32, (members, members), 1)).astype(F32)
    uppers, lowers, scales, sides = [], [], [], []
    for s in range(slots):
        total = (g0[s] + g1[s]) + (g2[s] + g3[s])
        gram, side = unpack_rows(total)
        system = gram + (members - 1.0) * eye
        square = jnp.sum(jnp.sum(system * system, axis=1, keepdims=True), axis=0, keepdims=True)
        scale = jnp.sqrt(square)
        uppers.append(system / scale)
        lowers.append(eye)
        scales.append(scale)
        sides.append(side)

    for step in range(ITERS):
        for s in range(slots):
            upper = split(uppers[s])
            if step == 0:
                middle = 1.5 * eye - 0.5 * uppers[s]
                lowers[s] = middle
                uppers[s] = dot3(upper, split(middle))
                continue
            lower = split(lowers[s])
            middle = split(1.5 * eye - 0.5 * dot3(lower, upper))
            lowers[s] = dot3(middle, lower)
            if step < ITERS - 1:
                uppers[s] = dot3(upper, middle)
    for s in range(slots):
        root = lowers[s] / jnp.sqrt(scales[s])
        parts = split(root)
        inner = dot3(split(sides[s]), parts, dot_nt)
        wmean = dot3(split(inner), parts, dot_nt)[0:1]
        out_ref[s] = (jnp.sqrt(jnp.float32(members - 1.0)) * root + wmean).astype(BF16)


def solve(gs, us, after):
    slots, _, members = gs[0].shape
    return pl.pallas_call(
        solve_kernel,
        in_specs=[vmem()] * 4 + [hbm() for _ in after],
        out_specs=vmem(),
        out_shape=jax.ShapeDtypeStruct((slots, members, members), BF16),
        compiler_params=params(24),
        cost_estimate=cost(us),
        name="newton_schulz",
    )(*gs, *after)


def apply_kernel(lev_ref, *rest):
    x_ref = rest[4]
    out_ref, x_buf, mixed_ref, out_buf, w_buf, x_sem, out_sem, w_sem = rest[-8:]
    weights = [pltpu.make_async_copy(rest[d], w_buf.at[d], w_sem.at[d]) for d in range(4)]
    fields, slots, members, cols = x_buf.shape
    groups, rows = out_buf.shape[1], out_buf.shape[2]
    per = slots // 4
    loads = [
        pltpu.make_async_copy(x_ref.at[f], x_buf.at[f], x_sem.at[f]) for f in range(fields)
    ]
    stores = [
        pltpu.make_async_copy(out_buf.at[f], out_ref.at[:, f], out_sem.at[f])
        for f in range(fields)
    ]
    start(weights)
    start(loads[:AHEAD])
    wait(weights)
    for f in range(fields):
        loads[f].wait()
        start(loads[f + AHEAD : f + AHEAD + 1])
        for d in range(4):
            owned = lax.rem(lev_ref[0] + 4 - d, 4) * per
            for s in range(per):
                x = x_buf[f, owned + s].astype(F32)
                mean = jnp.mean(x, axis=0, keepdims=True)
                mixed = dot(w_buf[d, s], (x - mean).astype(BF16))
                mixed_ref[owned + s] = mean + mixed
        moved = jnp.transpose(mixed_ref[...], (1, 0, 2)).reshape(groups, rows, cols)
        out_buf[f] = moved.astype(BF16)
        stores[f].start()
    wait(stores)


def apply(lev, ws, x, groups, us, mib, after):
    fields, slots, members, cols = x.shape
    rows = slots * members // groups
    return pl.pallas_call(
        apply_kernel,
        in_specs=[smem()] + [hbm()] * 5 + [hbm() for _ in after],
        out_specs=hbm(),
        out_shape=jax.ShapeDtypeStruct((groups, fields, rows, cols), BF16),
        scratch_shapes=[
            pltpu.VMEM((fields, slots, members, cols), BF16),
            pltpu.VMEM((slots, members, cols), F32),
            pltpu.VMEM((fields, groups, rows, cols), BF16),
            pltpu.VMEM((4,) + ws[0].shape, BF16),
            pltpu.SemaphoreType.DMA((fields,)),
            pltpu.SemaphoreType.DMA((fields,)),
            pltpu.SemaphoreType.DMA((4,)),
        ],
        compiler_params=params(mib),
        cost_estimate=cost(us),
        name="apply_weights",
    )(lev, *ws, x, *after)


def restore_kernel(order_ref, *refs):
    half = (len(refs) - 4) // 2
    recvs, out_ref, bufs = refs[:half], refs[half], refs[half + 1 : 2 * half + 1]
    out_buf, recv_sem, out_sem = refs[-3:]
    fields, members, patches, cols = out_buf.shape
    loads = [
        [
            pltpu.make_async_copy(r.at[:, f], b.at[f], recv_sem.at[f, c])
            for c, (r, b) in enumerate(zip(recvs, bufs))
        ]
        for f in range(fields)
    ]
    stores = [
        pltpu.make_async_copy(out_buf.at[f], out_ref.at[:, f], out_sem.at[f])
        for f in range(fields)
    ]
    for f in range(fields):
        start(loads[f])
    hot = slot_hot(order_ref).astype(BF16)
    for f in range(fields):
        wait(loads[f])
        blocks = [b[f].astype(F32) for b in bufs]
        for m in range(members):
            parts = []
            for block in blocks:
                slots = block.shape[1] // members
                parts.append(block[:, m * slots : (m + 1) * slots])
            stacked = jnp.concatenate(parts, axis=1).reshape(patches, cols).astype(BF16)
            out_buf[f, m] = dot(hot, stacked).astype(BF16)
        stores[f].start()
    wait(stores)


def restore(order, recvs, members):
    fields, cols = recvs[0].shape[1], recvs[0].shape[3]
    patches = order.shape[1]
    return pl.pallas_call(
        restore_kernel,
        in_specs=[vmem()] + [hbm()] * len(recvs),
        out_specs=hbm(),
        out_shape=jax.ShapeDtypeStruct((members, fields, patches, cols), BF16),
        scratch_shapes=[
            pltpu.VMEM((fields, r.shape[0], r.shape[2], cols), BF16) for r in recvs
        ]
        + [
            pltpu.VMEM((fields, members, patches, cols), BF16),
            pltpu.SemaphoreType.DMA((fields, len(recvs))),
            pltpu.SemaphoreType.DMA((fields,)),
        ],
        compiler_params=params(62),
        cost_estimate=cost(6),
        name="restore_order",
    )(order, *recvs)


def exchange(blocks):
    return [blocks[0]] + [
        lax.ppermute(blocks[d], "lev", [(i, (i + d) % 4) for i in range(4)]) for d in range(1, 4)
    ]


def body(background, patch_order, tile_counts, obs_column, obs_operator, obs_value, obs_weight):
    members_local, _, patches, fields, columns = background.shape
    slots_dev = tile_counts.shape[0]
    groups = patches // slots_dev
    tiles = obs_column.shape[0] // TILE
    level = lax.axis_index("lev")
    lev = jnp.reshape(level, (1,)).astype(jnp.int32)
    x = jnp.transpose(background[:, 0], (0, 2, 1, 3))
    order = patch_order.reshape(1, patches)
    col = obs_column.reshape(tiles, TILE)
    value = obs_value.reshape(tiles, TILE)
    weight = obs_weight.reshape(tiles, TILE)
    op = lax.dynamic_index_in_dim(obs_operator, level, 0, keepdims=False)
    op = jnp.transpose(op.reshape(fields, tiles, TILE), (1, 0, 2)).astype(F32)
    op = jnp.pad(op, ((0, 0), (0, 8 - fields), (0, 0)))

    gathered, firsts = [], []
    first = 0
    for slots in CHUNKS:
        if first > 0:
            order, op = lax.optimization_barrier((order, op))
        sent = send(order, x, first, slots, groups)
        gathered.append(lax.all_to_all(sent, "patch", split_axis=0, concat_axis=0, tiled=True))
        firsts.append(first)
        first += slots

    chunks = list(zip(CHUNKS, firsts, gathered))

    def see(c, us, after):
        slots, first, recv = chunks[c]
        room = tiles - (slots_dev - slots)
        x, *ys = observe(tile_counts, lev, recv, op, col, first, slots, room, us, (62, 62)[c], after)
        return x, ys

    def weigh(c, ys, us, after):
        slots, first, _ = chunks[c]
        return partial_gram(tile_counts, lev, ys, value, weight, first, slots, members, us, after)

    def analyse(x, w, us, mib, after):
        out = apply(lev, exchange([w] * 4), x, groups, us, mib, after)
        return out, lax.all_to_all(out, "patch", split_axis=0, concat_axis=0, tiled=True)

    members = members_local * groups
    x0, ys0 = see(0, 1, [sent])
    gs0 = weigh(0, exchange(ys0), 200, [])
    w0 = solve(exchange(gs0), 7, [])
    x1, ys1 = see(1, 20, [w0])
    out0, back0 = analyse(x0, w0, 100, 62, [ys1[0]])
    gs1 = weigh(1, exchange(ys1), 200, [out0])
    w1 = solve(exchange(gs1), 1, [])
    _, back1 = analyse(x1, w1, 1, 62, [])
    backs = [back0, back1]

    result = restore(order, backs, members_local)
    return jnp.transpose(result, (0, 2, 1, 3))[:, None]


def solution(mesh):
    in_specs = (
        P("patch", "lev", None, None, None),
        P(),
        P("patch"),
        P("patch"),
        P(None, None, "patch"),
        P("patch"),
        P("patch"),
    )
    out_specs = P("patch", "lev", None, None, None)
    return jax.shard_map(body, mesh=mesh, in_specs=in_specs, out_specs=out_specs, check_vma=False)
```

```python
import functools

import jax
import jax.numpy as jnp
from jax import lax
from jax.experimental import pallas as pl
from jax.experimental.pallas import tpu as pltpu
from jax.sharding import PartitionSpec as P

TILE = 128
ITERS = 10
CHUNKS = (8, 8)
F32 = jnp.float32
BF16 = jnp.bfloat16
AUG = 16
AHEAD = 3


def params(mib):
    return pltpu.CompilerParams(vmem_limit_bytes=mib * 1024 * 1024)


def cost(us):
    return pl.CostEstimate(flops=int(us * 1.15e9), bytes_accessed=0, transcendentals=0)


def vmem():
    return pl.BlockSpec(memory_space=pltpu.VMEM)


def hbm():
    return pl.BlockSpec(memory_space=pl.ANY)


def smem():
    return pl.BlockSpec(memory_space=pltpu.SMEM)


def dot(a, b):
    return jnp.dot(a, b, preferred_element_type=F32)


def dot_nt(a, b):
    return lax.dot_general(a, b, (((1,), (1,)), ((), ())), preferred_element_type=F32)


def split(a):
    hi = a.astype(BF16)
    return hi, (a - hi.astype(F32)).astype(BF16)


def dot3(a, b, mul=dot):
    ah, al = a
    bh, bl = b
    return mul(ah, bh) + (mul(ah, bl) + mul(al, bh))


def start(copies):
    for copy in copies:
        copy.start()


def wait(copies):
    for copy in copies:
        copy.wait()


def slot_hot(order_ref):
    patches = order_ref.shape[1]
    ids = lax.broadcasted_iota(jnp.int32, (patches, patches), 0)
    return (ids == order_ref[...]).astype(F32)


def send_kernel(first, order_ref, x_ref, out_ref, x_buf, out_buf, x_sem, out_sem):
    fields, members, patches, cols = x_buf.shape
    groups, rows = out_buf.shape[1], out_buf.shape[2]
    slots = rows // members
    loads = [
        pltpu.make_async_copy(x_ref.at[:, f], x_buf.at[f], x_sem.at[f]) for f in range(fields)
    ]
    stores = [
        pltpu.make_async_copy(out_buf.at[f], out_ref.at[:, f], out_sem.at[f])
        for f in range(fields)
    ]
    start(loads)
    hot = slot_hot(order_ref).T.reshape(groups, patches // groups, patches)
    hot = hot[:, first : first + slots].reshape(groups * slots, patches).astype(BF16)
    for f in range(fields):
        loads[f].wait()
        parts = [dot(hot, x_buf[f, m]).reshape(groups, slots, cols) for m in range(members)]
        out_buf[f] = jnp.concatenate(parts, axis=1).astype(BF16)
        stores[f].start()
    wait(stores)


def send(order, x, first, slots, groups):
    members, fields, patches, cols = x.shape
    return pl.pallas_call(
        functools.partial(send_kernel, first),
        in_specs=[vmem(), hbm()],
        out_specs=hbm(),
        out_shape=jax.ShapeDtypeStruct((groups, fields, members * slots, cols), BF16),
        scratch_shapes=[
            pltpu.VMEM((fields, members, patches, cols), BF16),
            pltpu.VMEM((fields, groups, members * slots, cols), BF16),
            pltpu.SemaphoreType.DMA((fields,)),
            pltpu.SemaphoreType.DMA((fields,)),
        ],
        compiler_params=params(62),
        cost_estimate=cost(5),
        name="send_permute",
    )(order, x)


def tile_range(base, count, lev):
    return lax.div(base - lev + 3, 4), lax.div(base + count - lev + 3, 4)


def observe_kernel(first, counts_ref, lev_ref, recv_ref, op_ref, col_ref, *rest):
    x_ref, y_refs, scratch = rest[-16], rest[-15:-11], rest[-11:]
    recv_buf, x_buf, op_buf, col_buf, mean_ref, y_buf, recv_sem, x_sem, op_sem, col_sem, y_sem = scratch
    fields, groups, rows, cols = recv_buf.shape
    slots, members = x_buf.shape[1], x_buf.shape[2]
    loads = [
        pltpu.make_async_copy(recv_ref.at[:, f], recv_buf.at[f], recv_sem.at[f])
        for f in range(fields)
    ]
    stores = [
        pltpu.make_async_copy(x_buf.at[f], x_ref.at[f], x_sem.at[f]) for f in range(fields)
    ]
    small = [
        pltpu.make_async_copy(op_ref, op_buf, op_sem),
        pltpu.make_async_copy(col_ref, col_buf, col_sem),
    ]
    start(loads)
    start(small)
    mean_ref[...] = jnp.zeros_like(mean_ref)
    for f in range(fields):
        loads[f].wait()
        block = recv_buf[f].astype(F32).reshape(members, slots, cols)
        x_buf[f] = jnp.transpose(block, (1, 0, 2)).astype(BF16)
        stores[f].start()
    wait(small)

    begin = jnp.int32(0)
    for s in range(first):
        begin = begin + counts_ref[s]
    column_ids = lax.broadcasted_iota(jnp.int32, (cols, TILE), 0)

    def table_of(row):
        hit = (column_ids == col_buf[pl.ds(row, 1), :]).astype(BF16)
        weights = op_buf[row]
        return jnp.concatenate(
            [hit * weights[f : f + 1, :].astype(BF16) for f in range(fields)], axis=0
        )

    def store(local, y, mean):
        offset = lax.rem(local + 4 - lev_ref[0], 4)
        place = lax.div(local, 4)
        mean_ref[offset, pl.ds(place, 1), :] = mean
        y_buf[offset, pl.ds(pl.multiple_of(place * members, members), members), :] = (
            y - mean
        ).astype(BF16)

    def slot_step(s, base):
        count = counts_ref[first + s]

        def observed(one, two):
            table = jnp.concatenate([table_of(begin + one), table_of(begin + two)], axis=1)
            x = jnp.concatenate([x_buf[f, s] for f in range(fields)], axis=1)
            y = dot(x, table)
            return y, jnp.mean(y, axis=0, keepdims=True)

        def store_both(one, two, result):
            y, mean = result
            store(one, y[:, :TILE], mean[:, :TILE])
            store(two, y[:, TILE:], mean[:, TILE:])

        def quad_step(i, carry):
            one = base + 4 * i
            results = observed(one, one + 1), observed(one + 2, one + 3)
            store_both(one, one + 1, results[0])
            store_both(one + 2, one + 3, results[1])
            return carry

        def oct_step(i, carry):
            ones = [base + 8 * i + 2 * n for n in range(4)]
            results = [observed(one, one + 1) for one in ones]
            for one, result in zip(ones, results):
                store_both(one, one + 1, result)
            return carry

        def pair_step(i, carry):
            one = base + 2 * i
            two = jnp.minimum(one + 1, base + count - 1)
            store_both(one, two, observed(one, two))
            return carry

        octs, quads = lax.div(count, 8), lax.div(count, 4)
        lax.fori_loop(0, octs, oct_step, 0)
        lax.fori_loop(2 * octs, quads, quad_step, 0)
        lax.fori_loop(2 * quads, lax.div(count + 1, 2), pair_step, 0)
        return base + count

    lax.fori_loop(0, slots, slot_step, jnp.int32(0))
    for d in range(4):
        mean = mean_ref[d]
        hi = mean.astype(BF16)
        mid = (mean - hi.astype(F32)).astype(BF16)
        low = (mean - hi.astype(F32) - mid.astype(F32)).astype(BF16)
        y_buf[d, y_buf.shape[1] - 48 :, :] = jnp.concatenate([hi, mid, low], axis=0)
    outs = [pltpu.make_async_copy(y_buf.at[d], y_refs[d], y_sem.at[d]) for d in range(4)]
    start(outs)
    wait(outs)
    wait(stores)


def observe(counts, lev, recv, op, col, first, slots, tiles, us, mib, after):
    groups, fields, rows, cols = recv.shape
    members = groups * rows // slots
    length = tiles // 4 * members + 48
    return pl.pallas_call(
        functools.partial(observe_kernel, first),
        in_specs=[smem(), smem(), hbm(), hbm(), hbm()] + [hbm() for _ in after],
        out_specs=[hbm()] * 5,
        out_shape=[jax.ShapeDtypeStruct((fields, slots, members, cols), BF16)]
        + [jax.ShapeDtypeStruct((length, TILE), BF16)] * 4,
        scratch_shapes=[
            pltpu.VMEM((fields, groups, rows, cols), BF16),
            pltpu.VMEM((fields, slots, members, cols), BF16),
            pltpu.VMEM(op.shape, F32),
            pltpu.VMEM(col.shape, jnp.int32),
            pltpu.VMEM((4, 16, TILE), F32),
            pltpu.VMEM((4, length, TILE), BF16),
            pltpu.SemaphoreType.DMA((fields,)),
            pltpu.SemaphoreType.DMA((fields,)),
            pltpu.SemaphoreType.DMA,
            pltpu.SemaphoreType.DMA,
            pltpu.SemaphoreType.DMA((4,)),
        ],
        compiler_params=params(mib),
        cost_estimate=cost(us),
        name="observe",
    )(counts, lev, recv, op, col, *after)


def pack_rows(a):
    half = a.shape[1] // 2
    quarter = half // 2
    left = lax.broadcasted_iota(jnp.int32, (quarter, 2 * half), 1) < half
    corner = jnp.where(left, a[:quarter], pltpu.roll(a[quarter:half], half, 1))
    return jnp.concatenate([corner, a[half : 2 * half + 8]], axis=0)


def unpack_rows(a):
    half = a.shape[1] // 2
    quarter = half // 2
    top = jnp.concatenate([a[:quarter], pltpu.roll(a[:quarter], half, 1)], axis=0)
    lower = jnp.concatenate([top, a[quarter : quarter + half]], axis=0)
    row = lax.broadcasted_iota(jnp.int32, lower.shape, 0)
    col = lax.broadcasted_iota(jnp.int32, lower.shape, 1)
    matrix = jnp.where((row < half) & (col >= half), lower.T, lower)
    return matrix, a[quarter + half :]


def gram_kernel(first, counts_ref, lev_ref, y0, y1, y2, y3, value_ref, weight_ref, *rest):
    out_refs, mean_ref, sum_ref = rest[-6:-2], rest[-2], rest[-1]
    per, _, members = out_refs[0].shape
    lev = lev_ref[0]
    start = jnp.int32(0)
    for s in range(first):
        start = start + counts_ref[s]
    tail = y0.shape[0] - 48
    total = (y0[tail:].astype(F32) + y1[tail:].astype(F32)) + (
        y2[tail:].astype(F32) + y3[tail:].astype(F32)
    )
    mean_ref[...] = total[0:16] + (total[16:32] + total[32:48])
    for d, out_ref in enumerate(out_refs):
        owned = lax.rem(lev + d, 4) * per
        base = lax.fori_loop(0, owned, lambda s, b: b + counts_ref[first + s], jnp.int32(0))
        for s in range(per):
            count = counts_ref[first + owned + s]
            sum_ref[...] = jnp.zeros_like(sum_ref)

            def tile_step(i, carry):
                row = start + 4 * i + lev
                rows = pl.ds(pl.multiple_of(i * members, members), members)
                pert = (y0[rows, :].astype(F32) + y1[rows, :].astype(F32)) + (
                    y2[rows, :].astype(F32) + y3[rows, :].astype(F32)
                )
                mean = mean_ref[pl.ds(i, 1), :]
                weight = weight_ref[pl.ds(row, 1), :]
                depart = value_ref[pl.ds(row, 1), :] - mean
                aug = jnp.concatenate([pert, depart, jnp.zeros((AUG - 1, TILE), F32)], axis=0)
                sum_ref[...] += dot3(split(aug * weight), split(pert), dot_nt)
                return carry

            low, high = tile_range(base, count, lev)
            lax.fori_loop(low, high, tile_step, 0)
            base = base + count
            out_ref[s] = pack_rows(sum_ref[...])


def partial_gram(counts, lev, ys, value, weight, first, slots, members, us, after):
    return pl.pallas_call(
        functools.partial(gram_kernel, first),
        in_specs=[smem(), smem()] + [vmem()] * 6 + [hbm() for _ in after],
        out_specs=[vmem()] * 4,
        out_shape=[jax.ShapeDtypeStruct((slots // 4, members * 3 // 4 + 8, members), F32)] * 4,
        scratch_shapes=[
            pltpu.VMEM((16, TILE), F32),
            pltpu.VMEM((members + AUG, members), F32),
        ],
        compiler_params=params(24),
        cost_estimate=cost(us),
        name="gram",
    )(counts, lev, *ys, value, weight, *after)


def solve_kernel(g0, g1, g2, g3, *rest):
    out_ref = rest[-1]
    slots, members = out_ref.shape[0], out_ref.shape[1]
    row = lax.broadcasted_iota(jnp.int32, (members, members), 0)
    eye = (row == lax.broadcasted_iota(jnp.int32, (members, members), 1)).astype(F32)
    uppers, lowers, scales, sides = [], [], [], []
    for s in range(slots):
        total = (g0[s] + g1[s]) + (g2[s] + g3[s])
        gram, side = unpack_rows(total)
        system = gram + (members - 1.0) * eye
        square = jnp.sum(jnp.sum(system * system, axis=1, keepdims=True), axis=0, keepdims=True)
        scale = jnp.sqrt(square)
        uppers.append(system / scale)
        lowers.append(eye)
        scales.append(scale)
        sides.append(side)

    for step in range(ITERS):
        for s in range(slots):
            upper = split(uppers[s])
            if step == 0:
                middle = 1.5 * eye - 0.5 * uppers[s]
                lowers[s] = middle
                uppers[s] = dot3(upper, split(middle))
                continue
            lower = split(lowers[s])
            middle = split(1.5 * eye - 0.5 * dot3(lower, upper))
            lowers[s] = dot3(middle, lower)
            if step < ITERS - 1:
                uppers[s] = dot3(upper, middle)
    for s in range(slots):
        root = lowers[s] / jnp.sqrt(scales[s])
        parts = split(root)
        inner = dot3(split(sides[s]), parts, dot_nt)
        wmean = dot3(split(inner), parts, dot_nt)[0:1]
        out_ref[s] = (jnp.sqrt(jnp.float32(members - 1.0)) * root + wmean).astype(BF16)


def solve(gs, us, after):
    slots, _, members = gs[0].shape
    return pl.pallas_call(
        solve_kernel,
        in_specs=[vmem()] * 4 + [hbm() for _ in after],
        out_specs=vmem(),
        out_shape=jax.ShapeDtypeStruct((slots, members, members), BF16),
        compiler_params=params(24),
        cost_estimate=cost(us),
        name="newton_schulz",
    )(*gs, *after)


def apply_kernel(lev_ref, *rest):
    x_ref = rest[4]
    out_ref, x_buf, mixed_ref, out_buf, w_buf, x_sem, out_sem, w_sem = rest[-8:]
    weights = [pltpu.make_async_copy(rest[d], w_buf.at[d], w_sem.at[d]) for d in range(4)]
    fields, slots, members, cols = x_buf.shape
    groups, rows = out_buf.shape[1], out_buf.shape[2]
    per = slots // 4
    loads = [
        pltpu.make_async_copy(x_ref.at[f], x_buf.at[f], x_sem.at[f]) for f in range(fields)
    ]
    stores = [
        pltpu.make_async_copy(out_buf.at[f], out_ref.at[:, f], out_sem.at[f])
        for f in range(fields)
    ]
    start(weights)
    start(loads[:AHEAD])
    wait(weights)
    for f in range(fields):
        loads[f].wait()
        start(loads[f + AHEAD : f + AHEAD + 1])
        for d in range(4):
            owned = lax.rem(lev_ref[0] + 4 - d, 4) * per
            for s in range(per):
                x = x_buf[f, owned + s].astype(F32)
                mean = jnp.mean(x, axis=0, keepdims=True)
                mixed = dot(w_buf[d, s], (x - mean).astype(BF16))
                mixed_ref[owned + s] = mean + mixed
        moved = jnp.transpose(mixed_ref[...], (1, 0, 2)).reshape(groups, rows, cols)
        out_buf[f] = moved.astype(BF16)
        stores[f].start()
    wait(stores)


def apply(lev, ws, x, groups, us, mib, after):
    fields, slots, members, cols = x.shape
    rows = slots * members // groups
    return pl.pallas_call(
        apply_kernel,
        in_specs=[smem()] + [hbm()] * 5 + [hbm() for _ in after],
        out_specs=hbm(),
        out_shape=jax.ShapeDtypeStruct((groups, fields, rows, cols), BF16),
        scratch_shapes=[
            pltpu.VMEM((fields, slots, members, cols), BF16),
            pltpu.VMEM((slots, members, cols), F32),
            pltpu.VMEM((fields, groups, rows, cols), BF16),
            pltpu.VMEM((4,) + ws[0].shape, BF16),
            pltpu.SemaphoreType.DMA((fields,)),
            pltpu.SemaphoreType.DMA((fields,)),
            pltpu.SemaphoreType.DMA((4,)),
        ],
        compiler_params=params(mib),
        cost_estimate=cost(us),
        name="apply_weights",
    )(lev, *ws, x, *after)


def restore_kernel(order_ref, *refs):
    half = (len(refs) - 4) // 2
    recvs, out_ref, bufs = refs[:half], refs[half], refs[half + 1 : 2 * half + 1]
    out_buf, recv_sem, out_sem = refs[-3:]
    fields, members, patches, cols = out_buf.shape
    loads = [
        [
            pltpu.make_async_copy(r.at[:, f], b.at[f], recv_sem.at[f, c])
            for c, (r, b) in enumerate(zip(recvs, bufs))
        ]
        for f in range(fields)
    ]
    stores = [
        pltpu.make_async_copy(out_buf.at[f], out_ref.at[:, f], out_sem.at[f])
        for f in range(fields)
    ]
    for f in range(fields):
        start(loads[f])
    hot = slot_hot(order_ref).astype(BF16)
    for f in range(fields):
        wait(loads[f])
        blocks = [b[f].astype(F32) for b in bufs]
        for m in range(members):
            parts = []
            for block in blocks:
                slots = block.shape[1] // members
                parts.append(block[:, m * slots : (m + 1) * slots])
            stacked = jnp.concatenate(parts, axis=1).reshape(patches, cols).astype(BF16)
            out_buf[f, m] = dot(hot, stacked).astype(BF16)
        stores[f].start()
    wait(stores)


def restore(order, recvs, members):
    fields, cols = recvs[0].shape[1], recvs[0].shape[3]
    patches = order.shape[1]
    return pl.pallas_call(
        restore_kernel,
        in_specs=[vmem()] + [hbm()] * len(recvs),
        out_specs=hbm(),
        out_shape=jax.ShapeDtypeStruct((members, fields, patches, cols), BF16),
        scratch_shapes=[
            pltpu.VMEM((fields, r.shape[0], r.shape[2], cols), BF16) for r in recvs
        ]
        + [
            pltpu.VMEM((fields, members, patches, cols), BF16),
            pltpu.SemaphoreType.DMA((fields, len(recvs))),
            pltpu.SemaphoreType.DMA((fields,)),
        ],
        compiler_params=params(40),
        cost_estimate=cost(6),
        name="restore_order",
    )(order, *recvs)


def exchange(blocks):
    return [blocks[0]] + [
        lax.ppermute(blocks[d], "lev", [(i, (i + d) % 4) for i in range(4)]) for d in range(1, 4)
    ]


def body(background, patch_order, tile_counts, obs_column, obs_operator, obs_value, obs_weight):
    members_local, _, patches, fields, columns = background.shape
    slots_dev = tile_counts.shape[0]
    groups = patches // slots_dev
    tiles = obs_column.shape[0] // TILE
    level = lax.axis_index("lev")
    lev = jnp.reshape(level, (1,)).astype(jnp.int32)
    x = jnp.transpose(background[:, 0], (0, 2, 1, 3))
    order = patch_order.reshape(1, patches)
    col = obs_column.reshape(tiles, TILE)
    value = obs_value.reshape(tiles, TILE)
    weight = obs_weight.reshape(tiles, TILE)
    op = lax.dynamic_index_in_dim(obs_operator, level, 0, keepdims=False)
    op = jnp.transpose(op.reshape(fields, tiles, TILE), (1, 0, 2)).astype(F32)
    op = jnp.pad(op, ((0, 0), (0, 8 - fields), (0, 0)))

    gathered, firsts = [], []
    first = 0
    for slots in CHUNKS:
        if first > 0:
            order, op = lax.optimization_barrier((order, op))
        sent = send(order, x, first, slots, groups)
        gathered.append(lax.all_to_all(sent, "patch", split_axis=0, concat_axis=0, tiled=True))
        firsts.append(first)
        first += slots

    chunks = list(zip(CHUNKS, firsts, gathered))

    def see(c, us, after):
        slots, first, recv = chunks[c]
        room = tiles - (slots_dev - slots)
        x, *ys = observe(tile_counts, lev, recv, op, col, first, slots, room, us, (62, 62)[c], after)
        return x, ys

    def weigh(c, ys, us, after):
        slots, first, _ = chunks[c]
        return partial_gram(tile_counts, lev, ys, value, weight, first, slots, members, us, after)

    def analyse(x, w, us, mib, after):
        out = apply(lev, exchange([w] * 4), x, groups, us, mib, after)
        return out, lax.all_to_all(out, "patch", split_axis=0, concat_axis=0, tiled=True)

    members = members_local * groups
    x0, ys0 = see(0, 1, [sent])
    gs0 = weigh(0, exchange(ys0), 200, [])
    w0 = solve(exchange(gs0), 7, [])
    x1, ys1 = see(1, 20, [w0])
    out0, back0 = analyse(x0, w0, 100, 62, [ys1[0]])
    gs1 = weigh(1, exchange(ys1), 200, [out0])
    w1 = solve(exchange(gs1), 1, [])
    _, back1 = analyse(x1, w1, 1, 62, [])
    backs = [back0, back1]

    result = restore(order, backs, members_local)
    return jnp.transpose(result, (0, 2, 1, 3))[:, None]


def solution(mesh):
    in_specs = (
        P("patch", "lev", None, None, None),
        P(),
        P("patch"),
        P("patch"),
        P(None, None, "patch"),
        P("patch"),
        P("patch"),
    )
    out_specs = P("patch", "lev", None, None, None)
    return jax.shard_map(body, mesh=mesh, in_specs=in_specs, out_specs=out_specs, check_vma=False)
```

```python
import functools

import jax
import jax.numpy as jnp
from jax import lax
from jax.experimental import pallas as pl
from jax.experimental.pallas import tpu as pltpu
from jax.sharding import PartitionSpec as P

TILE = 128
ITERS = 10
CHUNKS = (8, 8)
F32 = jnp.float32
BF16 = jnp.bfloat16
AUG = 16
AHEAD = 3


def params(mib):
    return pltpu.CompilerParams(vmem_limit_bytes=mib * 1024 * 1024)


def cost(us):
    return pl.CostEstimate(flops=int(us * 1.15e9), bytes_accessed=0, transcendentals=0)


def vmem():
    return pl.BlockSpec(memory_space=pltpu.VMEM)


def hbm():
    return pl.BlockSpec(memory_space=pl.ANY)


def smem():
    return pl.BlockSpec(memory_space=pltpu.SMEM)


def dot(a, b):
    return jnp.dot(a, b, preferred_element_type=F32)


def dot_nt(a, b):
    return lax.dot_general(a, b, (((1,), (1,)), ((), ())), preferred_element_type=F32)


def split(a):
    hi = a.astype(BF16)
    return hi, (a - hi.astype(F32)).astype(BF16)


def dot3(a, b, mul=dot):
    ah, al = a
    bh, bl = b
    return mul(ah, bh) + (mul(ah, bl) + mul(al, bh))


def start(copies):
    for copy in copies:
        copy.start()


def wait(copies):
    for copy in copies:
        copy.wait()


def slot_hot(order_ref):
    patches = order_ref.shape[1]
    ids = lax.broadcasted_iota(jnp.int32, (patches, patches), 0)
    return (ids == order_ref[...]).astype(F32)


def send_kernel(first, order_ref, x_ref, out_ref, x_buf, out_buf, x_sem, out_sem):
    fields, members, patches, cols = x_buf.shape
    groups, rows = out_buf.shape[1], out_buf.shape[2]
    slots = rows // members
    loads = [
        pltpu.make_async_copy(x_ref.at[:, f], x_buf.at[f], x_sem.at[f]) for f in range(fields)
    ]
    stores = [
        pltpu.make_async_copy(out_buf.at[f], out_ref.at[:, f], out_sem.at[f])
        for f in range(fields)
    ]
    start(loads)
    hot = slot_hot(order_ref).T.reshape(groups, patches // groups, patches)
    hot = hot[:, first : first + slots].reshape(groups * slots, patches).astype(BF16)
    for f in range(fields):
        loads[f].wait()
        parts = [dot(hot, x_buf[f, m]).reshape(groups, slots, cols) for m in range(members)]
        out_buf[f] = jnp.concatenate(parts, axis=1).astype(BF16)
        stores[f].start()
    wait(stores)


def send(order, x, first, slots, groups):
    members, fields, patches, cols = x.shape
    return pl.pallas_call(
        functools.partial(send_kernel, first),
        in_specs=[vmem(), hbm()],
        out_specs=hbm(),
        out_shape=jax.ShapeDtypeStruct((groups, fields, members * slots, cols), BF16),
        scratch_shapes=[
            pltpu.VMEM((fields, members, patches, cols), BF16),
            pltpu.VMEM((fields, groups, members * slots, cols), BF16),
            pltpu.SemaphoreType.DMA((fields,)),
            pltpu.SemaphoreType.DMA((fields,)),
        ],
        compiler_params=params(62),
        cost_estimate=cost(5),
        name="send_permute",
    )(order, x)


def tile_range(base, count, lev):
    return lax.div(base - lev + 3, 4), lax.div(base + count - lev + 3, 4)


def observe_kernel(first, counts_ref, lev_ref, recv_ref, op_ref, col_ref, *rest):
    x_ref, y_refs, scratch = rest[-16], rest[-15:-11], rest[-11:]
    recv_buf, x_buf, op_buf, col_buf, mean_ref, y_buf, recv_sem, x_sem, op_sem, col_sem, y_sem = scratch
    fields, groups, rows, cols = recv_buf.shape
    slots, members = x_buf.shape[1], x_buf.shape[2]
    loads = [
        pltpu.make_async_copy(recv_ref.at[:, f], recv_buf.at[f], recv_sem.at[f])
        for f in range(fields)
    ]
    stores = [
        pltpu.make_async_copy(x_buf.at[f], x_ref.at[f], x_sem.at[f]) for f in range(fields)
    ]
    small = [
        pltpu.make_async_copy(op_ref, op_buf, op_sem),
        pltpu.make_async_copy(col_ref, col_buf, col_sem),
    ]
    start(loads)
    start(small)
    mean_ref[...] = jnp.zeros_like(mean_ref)
    for f in range(fields):
        loads[f].wait()
        block = recv_buf[f].astype(F32).reshape(members, slots, cols)
        x_buf[f] = jnp.transpose(block, (1, 0, 2)).astype(BF16)
        stores[f].start()
    wait(small)

    begin = jnp.int32(0)
    for s in range(first):
        begin = begin + counts_ref[s]
    column_ids = lax.broadcasted_iota(jnp.int32, (cols, TILE), 0)

    def table_of(row):
        hit = (column_ids == col_buf[pl.ds(row, 1), :]).astype(BF16)
        weights = op_buf[row]
        return jnp.concatenate(
            [hit * weights[f : f + 1, :].astype(BF16) for f in range(fields)], axis=0
        )

    def store(local, y, mean):
        offset = lax.rem(local + 4 - lev_ref[0], 4)
        place = lax.div(local, 4)
        mean_ref[offset, pl.ds(place, 1), :] = mean
        y_buf[offset, pl.ds(pl.multiple_of(place * members, members), members), :] = (
            y - mean
        ).astype(BF16)

    def slot_step(s, base):
        count = counts_ref[first + s]

        def observed(one, two):
            table = jnp.concatenate([table_of(begin + one), table_of(begin + two)], axis=1)
            x = jnp.concatenate([x_buf[f, s] for f in range(fields)], axis=1)
            y = dot(x, table)
            return y, jnp.mean(y, axis=0, keepdims=True)

        def store_both(one, two, result):
            y, mean = result
            store(one, y[:, :TILE], mean[:, :TILE])
            store(two, y[:, TILE:], mean[:, TILE:])

        def quad_step(i, carry):
            one = base + 4 * i
            results = observed(one, one + 1), observed(one + 2, one + 3)
            store_both(one, one + 1, results[0])
            store_both(one + 2, one + 3, results[1])
            return carry

        def oct_step(i, carry):
            ones = [base + 8 * i + 2 * n for n in range(4)]
            results = [observed(one, one + 1) for one in ones]
            for one, result in zip(ones, results):
                store_both(one, one + 1, result)
            return carry

        def pair_step(i, carry):
            one = base + 2 * i
            two = jnp.minimum(one + 1, base + count - 1)
            store_both(one, two, observed(one, two))
            return carry

        octs, quads = lax.div(count, 8), lax.div(count, 4)
        lax.fori_loop(0, octs, oct_step, 0)
        lax.fori_loop(2 * octs, quads, quad_step, 0)
        lax.fori_loop(2 * quads, lax.div(count + 1, 2), pair_step, 0)
        return base + count

    lax.fori_loop(0, slots, slot_step, jnp.int32(0))
    for d in range(4):
        mean = mean_ref[d]
        hi = mean.astype(BF16)
        mid = (mean - hi.astype(F32)).astype(BF16)
        low = (mean - hi.astype(F32) - mid.astype(F32)).astype(BF16)
        y_buf[d, y_buf.shape[1] - 48 :, :] = jnp.concatenate([hi, mid, low], axis=0)
    outs = [pltpu.make_async_copy(y_buf.at[d], y_refs[d], y_sem.at[d]) for d in range(4)]
    start(outs)
    wait(outs)
    wait(stores)


def observe(counts, lev, recv, op, col, first, slots, tiles, us, mib, after):
    groups, fields, rows, cols = recv.shape
    members = groups * rows // slots
    length = tiles // 4 * members + 48
    return pl.pallas_call(
        functools.partial(observe_kernel, first),
        in_specs=[smem(), smem(), hbm(), hbm(), hbm()] + [hbm() for _ in after],
        out_specs=[hbm()] * 5,
        out_shape=[jax.ShapeDtypeStruct((fields, slots, members, cols), BF16)]
        + [jax.ShapeDtypeStruct((length, TILE), BF16)] * 4,
        scratch_shapes=[
            pltpu.VMEM((fields, groups, rows, cols), BF16),
            pltpu.VMEM((fields, slots, members, cols), BF16),
            pltpu.VMEM(op.shape, F32),
            pltpu.VMEM(col.shape, jnp.int32),
            pltpu.VMEM((4, 16, TILE), F32),
            pltpu.VMEM((4, length, TILE), BF16),
            pltpu.SemaphoreType.DMA((fields,)),
            pltpu.SemaphoreType.DMA((fields,)),
            pltpu.SemaphoreType.DMA,
            pltpu.SemaphoreType.DMA,
            pltpu.SemaphoreType.DMA((4,)),
        ],
        compiler_params=params(mib),
        cost_estimate=cost(us),
        name="observe",
    )(counts, lev, recv, op, col, *after)


def pack_rows(a):
    half = a.shape[1] // 2
    quarter = half // 2
    left = lax.broadcasted_iota(jnp.int32, (quarter, 2 * half), 1) < half
    corner = jnp.where(left, a[:quarter], pltpu.roll(a[quarter:half], half, 1))
    return jnp.concatenate([corner, a[half : 2 * half + 8]], axis=0)


def unpack_rows(a):
    half = a.shape[1] // 2
    quarter = half // 2
    top = jnp.concatenate([a[:quarter], pltpu.roll(a[:quarter], half, 1)], axis=0)
    lower = jnp.concatenate([top, a[quarter : quarter + half]], axis=0)
    row = lax.broadcasted_iota(jnp.int32, lower.shape, 0)
    col = lax.broadcasted_iota(jnp.int32, lower.shape, 1)
    matrix = jnp.where((row < half) & (col >= half), lower.T, lower)
    return matrix, a[quarter + half :]


def gram_kernel(first, counts_ref, lev_ref, y0, y1, y2, y3, value_ref, weight_ref, *rest):
    out_refs, mean_ref, sum_ref = rest[-6:-2], rest[-2], rest[-1]
    per, _, members = out_refs[0].shape
    lev = lev_ref[0]
    start = jnp.int32(0)
    for s in range(first):
        start = start + counts_ref[s]
    tail = y0.shape[0] - 48
    total = (y0[tail:].astype(F32) + y1[tail:].astype(F32)) + (
        y2[tail:].astype(F32) + y3[tail:].astype(F32)
    )
    mean_ref[...] = total[0:16] + (total[16:32] + total[32:48])
    for d, out_ref in enumerate(out_refs):
        owned = lax.rem(lev + d, 4) * per
        base = lax.fori_loop(0, owned, lambda s, b: b + counts_ref[first + s], jnp.int32(0))
        for s in range(per):
            count = counts_ref[first + owned + s]
            sum_ref[...] = jnp.zeros_like(sum_ref)

            def tile_step(i, carry):
                row = start + 4 * i + lev
                rows = pl.ds(pl.multiple_of(i * members, members), members)
                pert = (y0[rows, :].astype(F32) + y1[rows, :].astype(F32)) + (
                    y2[rows, :].astype(F32) + y3[rows, :].astype(F32)
                )
                mean = mean_ref[pl.ds(i, 1), :]
                weight = weight_ref[pl.ds(row, 1), :]
                depart = value_ref[pl.ds(row, 1), :] - mean
                aug = jnp.concatenate([pert, depart, jnp.zeros((AUG - 1, TILE), F32)], axis=0)
                sum_ref[...] += dot3(split(aug * weight), split(pert), dot_nt)
                return carry

            low, high = tile_range(base, count, lev)
            lax.fori_loop(low, high, tile_step, 0)
            base = base + count
            out_ref[s] = pack_rows(sum_ref[...])


def partial_gram(counts, lev, ys, value, weight, first, slots, members, us, after):
    return pl.pallas_call(
        functools.partial(gram_kernel, first),
        in_specs=[smem(), smem()] + [vmem()] * 6 + [hbm() for _ in after],
        out_specs=[vmem()] * 4,
        out_shape=[jax.ShapeDtypeStruct((slots // 4, members * 3 // 4 + 8, members), F32)] * 4,
        scratch_shapes=[
            pltpu.VMEM((16, TILE), F32),
            pltpu.VMEM((members + AUG, members), F32),
        ],
        compiler_params=params(24),
        cost_estimate=cost(us),
        name="gram",
    )(counts, lev, *ys, value, weight, *after)


def solve_kernel(g0, g1, g2, g3, *rest):
    out_ref = rest[-1]
    slots, members = out_ref.shape[0], out_ref.shape[1]
    row = lax.broadcasted_iota(jnp.int32, (members, members), 0)
    eye = (row == lax.broadcasted_iota(jnp.int32, (members, members), 1)).astype(F32)
    uppers, lowers, scales, sides = [], [], [], []
    for s in range(slots):
        total = (g0[s] + g1[s]) + (g2[s] + g3[s])
        gram, side = unpack_rows(total)
        system = gram + (members - 1.0) * eye
        square = jnp.sum(jnp.sum(system * system, axis=1, keepdims=True), axis=0, keepdims=True)
        scale = jnp.sqrt(square)
        uppers.append(system / scale)
        lowers.append(eye)
        scales.append(scale)
        sides.append(side)

    for step in range(ITERS):
        for s in range(slots):
            upper = split(uppers[s])
            if step == 0:
                middle = 1.5 * eye - 0.5 * uppers[s]
                lowers[s] = middle
                uppers[s] = dot3(upper, split(middle))
                continue
            lower = split(lowers[s])
            middle = split(1.5 * eye - 0.5 * dot3(lower, upper))
            lowers[s] = dot3(middle, lower)
            if step < ITERS - 1:
                uppers[s] = dot3(upper, middle)
    for s in range(slots):
        root = lowers[s] / jnp.sqrt(scales[s])
        parts = split(root)
        inner = dot3(split(sides[s]), parts, dot_nt)
        wmean = dot3(split(inner), parts, dot_nt)[0:1]
        out_ref[s] = (jnp.sqrt(jnp.float32(members - 1.0)) * root + wmean).astype(BF16)


def solve(gs, us, after):
    slots, _, members = gs[0].shape
    return pl.pallas_call(
        solve_kernel,
        in_specs=[vmem()] * 4 + [hbm() for _ in after],
        out_specs=vmem(),
        out_shape=jax.ShapeDtypeStruct((slots, members, members), BF16),
        compiler_params=params(24),
        cost_estimate=cost(us),
        name="newton_schulz",
    )(*gs, *after)


def apply_kernel(lev_ref, *rest):
    x_ref = rest[4]
    out_ref, x_buf, mixed_ref, out_buf, w_buf, x_sem, out_sem, w_sem = rest[-8:]
    weights = [pltpu.make_async_copy(rest[d], w_buf.at[d], w_sem.at[d]) for d in range(4)]
    fields, slots, members, cols = x_buf.shape
    groups, rows = out_buf.shape[1], out_buf.shape[2]
    per = slots // 4
    loads = [
        pltpu.make_async_copy(x_ref.at[f], x_buf.at[f], x_sem.at[f]) for f in range(fields)
    ]
    stores = [
        pltpu.make_async_copy(out_buf.at[f], out_ref.at[:, f], out_sem.at[f])
        for f in range(fields)
    ]
    start(weights)
    start(loads[:AHEAD])
    wait(weights)
    for f in range(fields):
        loads[f].wait()
        start(loads[f + AHEAD : f + AHEAD + 1])
        for d in range(4):
            owned = lax.rem(lev_ref[0] + 4 - d, 4) * per
            for s in range(per):
                x = x_buf[f, owned + s].astype(F32)
                mean = jnp.mean(x, axis=0, keepdims=True)
                mixed = dot(w_buf[d, s], (x - mean).astype(BF16))
                mixed_ref[owned + s] = mean + mixed
        moved = jnp.transpose(mixed_ref[...], (1, 0, 2)).reshape(groups, rows, cols)
        out_buf[f] = moved.astype(BF16)
        stores[f].start()
    wait(stores)


def apply(lev, ws, x, groups, us, mib, after):
    fields, slots, members, cols = x.shape
    rows = slots * members // groups
    return pl.pallas_call(
        apply_kernel,
        in_specs=[smem()] + [hbm()] * 5 + [hbm() for _ in after],
        out_specs=hbm(),
        out_shape=jax.ShapeDtypeStruct((groups, fields, rows, cols), BF16),
        scratch_shapes=[
            pltpu.VMEM((fields, slots, members, cols), BF16),
            pltpu.VMEM((slots, members, cols), F32),
            pltpu.VMEM((fields, groups, rows, cols), BF16),
            pltpu.VMEM((4,) + ws[0].shape, BF16),
            pltpu.SemaphoreType.DMA((fields,)),
            pltpu.SemaphoreType.DMA((fields,)),
            pltpu.SemaphoreType.DMA((4,)),
        ],
        compiler_params=params(mib),
        cost_estimate=cost(us),
        name="apply_weights",
    )(lev, *ws, x, *after)


def restore_kernel(order_ref, *refs):
    half = (len(refs) - 4) // 2
    recvs, out_ref, bufs = refs[:half], refs[half], refs[half + 1 : 2 * half + 1]
    out_buf, recv_sem, out_sem = refs[-3:]
    fields, members, patches, cols = out_buf.shape
    loads = [
        [
            pltpu.make_async_copy(r.at[:, f], b.at[f], recv_sem.at[f, c])
            for c, (r, b) in enumerate(zip(recvs, bufs))
        ]
        for f in range(fields)
    ]
    stores = [
        pltpu.make_async_copy(out_buf.at[f], out_ref.at[:, f], out_sem.at[f])
        for f in range(fields)
    ]
    for f in range(fields):
        start(loads[f])
    hot = slot_hot(order_ref).astype(BF16)
    for f in range(fields):
        wait(loads[f])
        blocks = [b[f].astype(F32) for b in bufs]
        for m in range(members):
            parts = []
            for block in blocks:
                slots = block.shape[1] // members
                parts.append(block[:, m * slots : (m + 1) * slots])
            stacked = jnp.concatenate(parts, axis=1).reshape(patches, cols).astype(BF16)
            out_buf[f, m] = dot(hot, stacked).astype(BF16)
        stores[f].start()
    wait(stores)


def restore(order, recvs, members):
    fields, cols = recvs[0].shape[1], recvs[0].shape[3]
    patches = order.shape[1]
    return pl.pallas_call(
        restore_kernel,
        in_specs=[vmem()] + [hbm()] * len(recvs),
        out_specs=hbm(),
        out_shape=jax.ShapeDtypeStruct((members, fields, patches, cols), BF16),
        scratch_shapes=[
            pltpu.VMEM((fields, r.shape[0], r.shape[2], cols), BF16) for r in recvs
        ]
        + [
            pltpu.VMEM((fields, members, patches, cols), BF16),
            pltpu.SemaphoreType.DMA((fields, len(recvs))),
            pltpu.SemaphoreType.DMA((fields,)),
        ],
        compiler_params=params(40),
        cost_estimate=cost(6),
        name="restore_order",
    )(order, *recvs)


def exchange(blocks):
    return [blocks[0]] + [
        lax.ppermute(blocks[d], "lev", [(i, (i + d) % 4) for i in range(4)]) for d in range(1, 4)
    ]


def body(background, patch_order, tile_counts, obs_column, obs_operator, obs_value, obs_weight):
    members_local, _, patches, fields, columns = background.shape
    slots_dev = tile_counts.shape[0]
    groups = patches // slots_dev
    tiles = obs_column.shape[0] // TILE
    level = lax.axis_index("lev")
    lev = jnp.reshape(level, (1,)).astype(jnp.int32)
    x = jnp.transpose(background[:, 0], (0, 2, 1, 3))
    order = patch_order.reshape(1, patches)
    col = obs_column.reshape(tiles, TILE)
    value = obs_value.reshape(tiles, TILE)
    weight = obs_weight.reshape(tiles, TILE)
    op = lax.dynamic_index_in_dim(obs_operator, level, 0, keepdims=False)
    op = jnp.transpose(op.reshape(fields, tiles, TILE), (1, 0, 2)).astype(F32)
    op = jnp.pad(op, ((0, 0), (0, 8 - fields), (0, 0)))

    gathered, firsts = [], []
    first = 0
    for slots in CHUNKS:
        if first > 0:
            order, op = lax.optimization_barrier((order, op))
        sent = send(order, x, first, slots, groups)
        gathered.append(lax.all_to_all(sent, "patch", split_axis=0, concat_axis=0, tiled=True))
        firsts.append(first)
        first += slots

    chunks = list(zip(CHUNKS, firsts, gathered))

    def see(c, us, after):
        slots, first, recv = chunks[c]
        room = tiles - (slots_dev - slots)
        x, *ys = observe(tile_counts, lev, recv, op, col, first, slots, room, us, (62, 62)[c], after)
        return x, ys

    def weigh(c, ys, us, after):
        slots, first, _ = chunks[c]
        return partial_gram(tile_counts, lev, ys, value, weight, first, slots, members, us, after)

    def analyse(x, w, us, mib, after):
        out = apply(lev, exchange([w] * 4), x, groups, us, mib, after)
        return out, lax.all_to_all(out, "patch", split_axis=0, concat_axis=0, tiled=True)

    members = members_local * groups
    x0, ys0 = see(0, 1, [sent])
    gs0 = weigh(0, exchange(ys0), 200, [])
    w0 = solve(exchange(gs0), 7, [])
    x1, ys1 = see(1, 20, [w0])
    out0, back0 = analyse(x0, w0, 100, 62, [ys1[0]])
    gs1 = weigh(1, exchange(ys1), 200, [out0])
    w1 = solve(exchange(gs1), 1, [])
    _, back1 = analyse(x1, w1, 1, 48, [])
    backs = [back0, back1]

    result = restore(order, backs, members_local)
    return jnp.transpose(result, (0, 2, 1, 3))[:, None]


def solution(mesh):
    in_specs = (
        P("patch", "lev", None, None, None),
        P(),
        P("patch"),
        P("patch"),
        P(None, None, "patch"),
        P("patch"),
        P("patch"),
    )
    out_specs = P("patch", "lev", None, None, None)
    return jax.shard_map(body, mesh=mesh, in_specs=in_specs, out_specs=out_specs, check_vma=False)
```

```python
import functools

import jax
import jax.numpy as jnp
from jax import lax
from jax.experimental import pallas as pl
from jax.experimental.pallas import tpu as pltpu
from jax.sharding import PartitionSpec as P

TILE = 128
ITERS = 10
CHUNKS = (8, 8)
F32 = jnp.float32
BF16 = jnp.bfloat16
AUG = 16
AHEAD = 3


def params(mib):
    return pltpu.CompilerParams(vmem_limit_bytes=mib * 1024 * 1024)


def cost(us):
    return pl.CostEstimate(flops=int(us * 1.15e9), bytes_accessed=0, transcendentals=0)


def vmem():
    return pl.BlockSpec(memory_space=pltpu.VMEM)


def hbm():
    return pl.BlockSpec(memory_space=pl.ANY)


def smem():
    return pl.BlockSpec(memory_space=pltpu.SMEM)


def dot(a, b):
    return jnp.dot(a, b, preferred_element_type=F32)


def dot_nt(a, b):
    return lax.dot_general(a, b, (((1,), (1,)), ((), ())), preferred_element_type=F32)


def split(a):
    hi = a.astype(BF16)
    return hi, (a - hi.astype(F32)).astype(BF16)


def dot3(a, b, mul=dot):
    ah, al = a
    bh, bl = b
    return mul(ah, bh) + (mul(ah, bl) + mul(al, bh))


def start(copies):
    for copy in copies:
        copy.start()


def wait(copies):
    for copy in copies:
        copy.wait()


def slot_hot(order_ref):
    patches = order_ref.shape[1]
    ids = lax.broadcasted_iota(jnp.int32, (patches, patches), 0)
    return (ids == order_ref[...]).astype(F32)


def send_kernel(first, order_ref, x_ref, out_ref, x_buf, out_buf, x_sem, out_sem):
    fields, members, patches, cols = x_buf.shape
    groups, rows = out_buf.shape[1], out_buf.shape[2]
    slots = rows // members
    loads = [
        pltpu.make_async_copy(x_ref.at[:, f], x_buf.at[f], x_sem.at[f]) for f in range(fields)
    ]
    stores = [
        pltpu.make_async_copy(out_buf.at[f], out_ref.at[:, f], out_sem.at[f])
        for f in range(fields)
    ]
    start(loads)
    hot = slot_hot(order_ref).T.reshape(groups, patches // groups, patches)
    hot = hot[:, first : first + slots].reshape(groups * slots, patches).astype(BF16)
    for f in range(fields):
        loads[f].wait()
        parts = [dot(hot, x_buf[f, m]).reshape(groups, slots, cols) for m in range(members)]
        out_buf[f] = jnp.concatenate(parts, axis=1).astype(BF16)
        stores[f].start()
    wait(stores)


def send(order, x, first, slots, groups):
    members, fields, patches, cols = x.shape
    return pl.pallas_call(
        functools.partial(send_kernel, first),
        in_specs=[vmem(), hbm()],
        out_specs=hbm(),
        out_shape=jax.ShapeDtypeStruct((groups, fields, members * slots, cols), BF16),
        scratch_shapes=[
            pltpu.VMEM((fields, members, patches, cols), BF16),
            pltpu.VMEM((fields, groups, members * slots, cols), BF16),
            pltpu.SemaphoreType.DMA((fields,)),
            pltpu.SemaphoreType.DMA((fields,)),
        ],
        compiler_params=params(62),
        cost_estimate=cost(5),
        name="send_permute",
    )(order, x)


def tile_range(base, count, lev):
    return lax.div(base - lev + 3, 4), lax.div(base + count - lev + 3, 4)


def observe_kernel(first, counts_ref, lev_ref, recv_ref, op_ref, col_ref, *rest):
    x_ref, y_refs, scratch = rest[-16], rest[-15:-11], rest[-11:]
    recv_buf, x_buf, op_buf, col_buf, mean_ref, y_buf, recv_sem, x_sem, op_sem, col_sem, y_sem = scratch
    fields, groups, rows, cols = recv_buf.shape
    slots, members = x_buf.shape[1], x_buf.shape[2]
    loads = [
        pltpu.make_async_copy(recv_ref.at[:, f], recv_buf.at[f], recv_sem.at[f])
        for f in range(fields)
    ]
    stores = [
        pltpu.make_async_copy(x_buf.at[f], x_ref.at[f], x_sem.at[f]) for f in range(fields)
    ]
    small = [
        pltpu.make_async_copy(op_ref, op_buf, op_sem),
        pltpu.make_async_copy(col_ref, col_buf, col_sem),
    ]
    start(loads)
    start(small)
    mean_ref[...] = jnp.zeros_like(mean_ref)
    for f in range(fields):
        loads[f].wait()
        block = recv_buf[f].astype(F32).reshape(members, slots, cols)
        x_buf[f] = jnp.transpose(block, (1, 0, 2)).astype(BF16)
        stores[f].start()
    wait(small)

    begin = jnp.int32(0)
    for s in range(first):
        begin = begin + counts_ref[s]
    column_ids = lax.broadcasted_iota(jnp.int32, (cols, TILE), 0)

    def table_of(row):
        hit = (column_ids == col_buf[pl.ds(row, 1), :]).astype(BF16)
        weights = op_buf[row]
        return jnp.concatenate(
            [hit * weights[f : f + 1, :].astype(BF16) for f in range(fields)], axis=0
        )

    def store(local, y, mean):
        offset = lax.rem(local + 4 - lev_ref[0], 4)
        place = lax.div(local, 4)
        mean_ref[offset, pl.ds(place, 1), :] = mean
        y_buf[offset, pl.ds(pl.multiple_of(place * members, members), members), :] = (
            y - mean
        ).astype(BF16)

    def slot_step(s, base):
        count = counts_ref[first + s]

        def observed(one, two):
            table = jnp.concatenate([table_of(begin + one), table_of(begin + two)], axis=1)
            x = jnp.concatenate([x_buf[f, s] for f in range(fields)], axis=1)
            y = dot(x, table)
            return y, jnp.mean(y, axis=0, keepdims=True)

        def store_both(one, two, result):
            y, mean = result
            store(one, y[:, :TILE], mean[:, :TILE])
            store(two, y[:, TILE:], mean[:, TILE:])

        def quad_step(i, carry):
            one = base + 4 * i
            results = observed(one, one + 1), observed(one + 2, one + 3)
            store_both(one, one + 1, results[0])
            store_both(one + 2, one + 3, results[1])
            return carry

        def oct_step(i, carry):
            ones = [base + 8 * i + 2 * n for n in range(4)]
            results = [observed(one, one + 1) for one in ones]
            for one, result in zip(ones, results):
                store_both(one, one + 1, result)
            return carry

        def pair_step(i, carry):
            one = base + 2 * i
            two = jnp.minimum(one + 1, base + count - 1)
            store_both(one, two, observed(one, two))
            return carry

        octs, quads = lax.div(count, 8), lax.div(count, 4)
        lax.fori_loop(0, octs, oct_step, 0)
        lax.fori_loop(2 * octs, quads, quad_step, 0)
        lax.fori_loop(2 * quads, lax.div(count + 1, 2), pair_step, 0)
        return base + count

    lax.fori_loop(0, slots, slot_step, jnp.int32(0))
    outs = [pltpu.make_async_copy(y_buf.at[d], y_refs[d], y_sem.at[d]) for d in range(4)]
    for d in range(4):
        mean = mean_ref[d]
        hi = mean.astype(BF16)
        mid = (mean - hi.astype(F32)).astype(BF16)
        low = (mean - hi.astype(F32) - mid.astype(F32)).astype(BF16)
        y_buf[d, y_buf.shape[1] - 48 :, :] = jnp.concatenate([hi, mid, low], axis=0)
        outs[d].start()
    wait(outs)
    wait(stores)


def observe(counts, lev, recv, op, col, first, slots, tiles, us, mib, after):
    groups, fields, rows, cols = recv.shape
    members = groups * rows // slots
    length = tiles // 4 * members + 48
    return pl.pallas_call(
        functools.partial(observe_kernel, first),
        in_specs=[smem(), smem(), hbm(), hbm(), hbm()] + [hbm() for _ in after],
        out_specs=[hbm()] * 5,
        out_shape=[jax.ShapeDtypeStruct((fields, slots, members, cols), BF16)]
        + [jax.ShapeDtypeStruct((length, TILE), BF16)] * 4,
        scratch_shapes=[
            pltpu.VMEM((fields, groups, rows, cols), BF16),
            pltpu.VMEM((fields, slots, members, cols), BF16),
            pltpu.VMEM(op.shape, F32),
            pltpu.VMEM(col.shape, jnp.int32),
            pltpu.VMEM((4, 16, TILE), F32),
            pltpu.VMEM((4, length, TILE), BF16),
            pltpu.SemaphoreType.DMA((fields,)),
            pltpu.SemaphoreType.DMA((fields,)),
            pltpu.SemaphoreType.DMA,
            pltpu.SemaphoreType.DMA,
            pltpu.SemaphoreType.DMA((4,)),
        ],
        compiler_params=params(mib),
        cost_estimate=cost(us),
        name="observe",
    )(counts, lev, recv, op, col, *after)


def pack_rows(a):
    half = a.shape[1] // 2
    quarter = half // 2
    left = lax.broadcasted_iota(jnp.int32, (quarter, 2 * half), 1) < half
    corner = jnp.where(left, a[:quarter], pltpu.roll(a[quarter:half], half, 1))
    return jnp.concatenate([corner, a[half : 2 * half + 8]], axis=0)


def unpack_rows(a):
    half = a.shape[1] // 2
    quarter = half // 2
    top = jnp.concatenate([a[:quarter], pltpu.roll(a[:quarter], half, 1)], axis=0)
    lower = jnp.concatenate([top, a[quarter : quarter + half]], axis=0)
    row = lax.broadcasted_iota(jnp.int32, lower.shape, 0)
    col = lax.broadcasted_iota(jnp.int32, lower.shape, 1)
    matrix = jnp.where((row < half) & (col >= half), lower.T, lower)
    return matrix, a[quarter + half :]


def gram_kernel(first, counts_ref, lev_ref, y0, y1, y2, y3, value_ref, weight_ref, *rest):
    out_refs, mean_ref, sum_ref = rest[-6:-2], rest[-2], rest[-1]
    per, _, members = out_refs[0].shape
    lev = lev_ref[0]
    start = jnp.int32(0)
    for s in range(first):
        start = start + counts_ref[s]
    tail = y0.shape[0] - 48
    total = (y0[tail:].astype(F32) + y1[tail:].astype(F32)) + (
        y2[tail:].astype(F32) + y3[tail:].astype(F32)
    )
    mean_ref[...] = total[0:16] + (total[16:32] + total[32:48])
    for d, out_ref in enumerate(out_refs):
        owned = lax.rem(lev + d, 4) * per
        base = lax.fori_loop(0, owned, lambda s, b: b + counts_ref[first + s], jnp.int32(0))
        for s in range(per):
            count = counts_ref[first + owned + s]
            sum_ref[...] = jnp.zeros_like(sum_ref)

            def tile_step(i, carry):
                row = start + 4 * i + lev
                rows = pl.ds(pl.multiple_of(i * members, members), members)
                pert = (y0[rows, :].astype(F32) + y1[rows, :].astype(F32)) + (
                    y2[rows, :].astype(F32) + y3[rows, :].astype(F32)
                )
                mean = mean_ref[pl.ds(i, 1), :]
                weight = weight_ref[pl.ds(row, 1), :]
                depart = value_ref[pl.ds(row, 1), :] - mean
                aug = jnp.concatenate([pert, depart, jnp.zeros((AUG - 1, TILE), F32)], axis=0)
                sum_ref[...] += dot3(split(aug * weight), split(pert), dot_nt)
                return carry

            low, high = tile_range(base, count, lev)
            lax.fori_loop(low, high, tile_step, 0)
            base = base + count
            out_ref[s] = pack_rows(sum_ref[...])


def partial_gram(counts, lev, ys, value, weight, first, slots, members, us, after):
    return pl.pallas_call(
        functools.partial(gram_kernel, first),
        in_specs=[smem(), smem()] + [vmem()] * 6 + [hbm() for _ in after],
        out_specs=[vmem()] * 4,
        out_shape=[jax.ShapeDtypeStruct((slots // 4, members * 3 // 4 + 8, members), F32)] * 4,
        scratch_shapes=[
            pltpu.VMEM((16, TILE), F32),
            pltpu.VMEM((members + AUG, members), F32),
        ],
        compiler_params=params(24),
        cost_estimate=cost(us),
        name="gram",
    )(counts, lev, *ys, value, weight, *after)


def solve_kernel(g0, g1, g2, g3, *rest):
    out_ref = rest[-1]
    slots, members = out_ref.shape[0], out_ref.shape[1]
    row = lax.broadcasted_iota(jnp.int32, (members, members), 0)
    eye = (row == lax.broadcasted_iota(jnp.int32, (members, members), 1)).astype(F32)
    uppers, lowers, scales, sides = [], [], [], []
    for s in range(slots):
        total = (g0[s] + g1[s]) + (g2[s] + g3[s])
        gram, side = unpack_rows(total)
        system = gram + (members - 1.0) * eye
        square = jnp.sum(jnp.sum(system * system, axis=1, keepdims=True), axis=0, keepdims=True)
        scale = jnp.sqrt(square)
        uppers.append(system / scale)
        lowers.append(eye)
        scales.append(scale)
        sides.append(side)

    for step in range(ITERS):
        for s in range(slots):
            upper = split(uppers[s])
            if step == 0:
                middle = 1.5 * eye - 0.5 * uppers[s]
                lowers[s] = middle
                uppers[s] = dot3(upper, split(middle))
                continue
            lower = split(lowers[s])
            middle = split(1.5 * eye - 0.5 * dot3(lower, upper))
            lowers[s] = dot3(middle, lower)
            if step < ITERS - 1:
                uppers[s] = dot3(upper, middle)
    for s in range(slots):
        root = lowers[s] / jnp.sqrt(scales[s])
        parts = split(root)
        inner = dot3(split(sides[s]), parts, dot_nt)
        wmean = dot3(split(inner), parts, dot_nt)[0:1]
        out_ref[s] = (jnp.sqrt(jnp.float32(members - 1.0)) * root + wmean).astype(BF16)


def solve(gs, us, after):
    slots, _, members = gs[0].shape
    return pl.pallas_call(
        solve_kernel,
        in_specs=[vmem()] * 4 + [hbm() for _ in after],
        out_specs=vmem(),
        out_shape=jax.ShapeDtypeStruct((slots, members, members), BF16),
        compiler_params=params(24),
        cost_estimate=cost(us),
        name="newton_schulz",
    )(*gs, *after)


def apply_kernel(lev_ref, *rest):
    x_ref = rest[4]
    out_ref, x_buf, mixed_ref, out_buf, w_buf, x_sem, out_sem, w_sem = rest[-8:]
    weights = [pltpu.make_async_copy(rest[d], w_buf.at[d], w_sem.at[d]) for d in range(4)]
    fields, slots, members, cols = x_buf.shape
    groups, rows = out_buf.shape[1], out_buf.shape[2]
    per = slots // 4
    loads = [
        pltpu.make_async_copy(x_ref.at[f], x_buf.at[f], x_sem.at[f]) for f in range(fields)
    ]
    stores = [
        pltpu.make_async_copy(out_buf.at[f], out_ref.at[:, f], out_sem.at[f])
        for f in range(fields)
    ]
    start(weights)
    start(loads[:AHEAD])
    wait(weights)
    for f in range(fields):
        loads[f].wait()
        start(loads[f + AHEAD : f + AHEAD + 1])
        for d in range(4):
            owned = lax.rem(lev_ref[0] + 4 - d, 4) * per
            for s in range(per):
                x = x_buf[f, owned + s].astype(F32)
                mean = jnp.mean(x, axis=0, keepdims=True)
                mixed = dot(w_buf[d, s], (x - mean).astype(BF16))
                mixed_ref[owned + s] = mean + mixed
        moved = jnp.transpose(mixed_ref[...], (1, 0, 2)).reshape(groups, rows, cols)
        out_buf[f] = moved.astype(BF16)
        stores[f].start()
    wait(stores)


def apply(lev, ws, x, groups, us, mib, after):
    fields, slots, members, cols = x.shape
    rows = slots * members // groups
    return pl.pallas_call(
        apply_kernel,
        in_specs=[smem()] + [hbm()] * 5 + [hbm() for _ in after],
        out_specs=hbm(),
        out_shape=jax.ShapeDtypeStruct((groups, fields, rows, cols), BF16),
        scratch_shapes=[
            pltpu.VMEM((fields, slots, members, cols), BF16),
            pltpu.VMEM((slots, members, cols), F32),
            pltpu.VMEM((fields, groups, rows, cols), BF16),
            pltpu.VMEM((4,) + ws[0].shape, BF16),
            pltpu.SemaphoreType.DMA((fields,)),
            pltpu.SemaphoreType.DMA((fields,)),
            pltpu.SemaphoreType.DMA((4,)),
        ],
        compiler_params=params(mib),
        cost_estimate=cost(us),
        name="apply_weights",
    )(lev, *ws, x, *after)


def restore_kernel(order_ref, *refs):
    half = (len(refs) - 4) // 2
    recvs, out_ref, bufs = refs[:half], refs[half], refs[half + 1 : 2 * half + 1]
    out_buf, recv_sem, out_sem = refs[-3:]
    fields, members, patches, cols = out_buf.shape
    loads = [
        [
            pltpu.make_async_copy(r.at[:, f], b.at[f], recv_sem.at[f, c])
            for c, (r, b) in enumerate(zip(recvs, bufs))
        ]
        for f in range(fields)
    ]
    stores = [
        pltpu.make_async_copy(out_buf.at[f], out_ref.at[:, f], out_sem.at[f])
        for f in range(fields)
    ]
    for f in range(fields):
        start(loads[f])
    hot = slot_hot(order_ref).astype(BF16)
    for f in range(fields):
        wait(loads[f])
        blocks = [b[f].astype(F32) for b in bufs]
        for m in range(members):
            parts = []
            for block in blocks:
                slots = block.shape[1] // members
                parts.append(block[:, m * slots : (m + 1) * slots])
            stacked = jnp.concatenate(parts, axis=1).reshape(patches, cols).astype(BF16)
            out_buf[f, m] = dot(hot, stacked).astype(BF16)
        stores[f].start()
    wait(stores)


def restore(order, recvs, members):
    fields, cols = recvs[0].shape[1], recvs[0].shape[3]
    patches = order.shape[1]
    return pl.pallas_call(
        restore_kernel,
        in_specs=[vmem()] + [hbm()] * len(recvs),
        out_specs=hbm(),
        out_shape=jax.ShapeDtypeStruct((members, fields, patches, cols), BF16),
        scratch_shapes=[
            pltpu.VMEM((fields, r.shape[0], r.shape[2], cols), BF16) for r in recvs
        ]
        + [
            pltpu.VMEM((fields, members, patches, cols), BF16),
            pltpu.SemaphoreType.DMA((fields, len(recvs))),
            pltpu.SemaphoreType.DMA((fields,)),
        ],
        compiler_params=params(40),
        cost_estimate=cost(6),
        name="restore_order",
    )(order, *recvs)


def exchange(blocks):
    came = {0: blocks[0]}
    for d in (2, 1, 3):
        came[d] = lax.ppermute(blocks[d], "lev", [(i, (i + d) % 4) for i in range(4)])
    return [came[d] for d in range(4)]


def body(background, patch_order, tile_counts, obs_column, obs_operator, obs_value, obs_weight):
    members_local, _, patches, fields, columns = background.shape
    slots_dev = tile_counts.shape[0]
    groups = patches // slots_dev
    tiles = obs_column.shape[0] // TILE
    level = lax.axis_index("lev")
    lev = jnp.reshape(level, (1,)).astype(jnp.int32)
    x = jnp.transpose(background[:, 0], (0, 2, 1, 3))
    order = patch_order.reshape(1, patches)
    col = obs_column.reshape(tiles, TILE)
    value = obs_value.reshape(tiles, TILE)
    weight = obs_weight.reshape(tiles, TILE)
    op = lax.dynamic_index_in_dim(obs_operator, level, 0, keepdims=False)
    op = jnp.transpose(op.reshape(fields, tiles, TILE), (1, 0, 2)).astype(F32)
    op = jnp.pad(op, ((0, 0), (0, 8 - fields), (0, 0)))

    gathered, firsts = [], []
    first = 0
    for slots in CHUNKS:
        if first > 0:
            order, op = lax.optimization_barrier((order, op))
        sent = send(order, x, first, slots, groups)
        gathered.append(lax.all_to_all(sent, "patch", split_axis=0, concat_axis=0, tiled=True))
        firsts.append(first)
        first += slots

    chunks = list(zip(CHUNKS, firsts, gathered))

    def see(c, us, after):
        slots, first, recv = chunks[c]
        room = tiles - (slots_dev - slots)
        x, *ys = observe(tile_counts, lev, recv, op, col, first, slots, room, us, (62, 62)[c], after)
        return x, ys

    def weigh(c, ys, us, after):
        slots, first, _ = chunks[c]
        return partial_gram(tile_counts, lev, ys, value, weight, first, slots, members, us, after)

    def analyse(x, w, us, mib, after):
        out = apply(lev, exchange([w] * 4), x, groups, us, mib, after)
        return out, lax.all_to_all(out, "patch", split_axis=0, concat_axis=0, tiled=True)

    members = members_local * groups
    x0, ys0 = see(0, 1, [sent])
    gs0 = weigh(0, exchange(ys0), 200, [])
    w0 = solve(exchange(gs0), 7, [])
    x1, ys1 = see(1, 20, [w0])
    out0, back0 = analyse(x0, w0, 100, 62, [ys1[0]])
    gs1 = weigh(1, exchange(ys1), 200, [out0])
    w1 = solve(exchange(gs1), 1, [])
    _, back1 = analyse(x1, w1, 1, 62, [])
    backs = [back0, back1]

    result = restore(order, backs, members_local)
    return jnp.transpose(result, (0, 2, 1, 3))[:, None]


def solution(mesh):
    in_specs = (
        P("patch", "lev", None, None, None),
        P(),
        P("patch"),
        P("patch"),
        P(None, None, "patch"),
        P("patch"),
        P("patch"),
    )
    out_specs = P("patch", "lev", None, None, None)
    return jax.shard_map(body, mesh=mesh, in_specs=in_specs, out_specs=out_specs, check_vma=False)
```
